1024 devices in a mesh: ep: 64 (over x, y), tp: 16 (over z, core).
Axes of the slice: x: 8, y: 8, z: 8, core: 2. Of those that a mesh axis runs over, the one named last changes fastest.
Arguments:
- tokens: bfloat16 [2048, 4096], P('ep', 'tp'), may hold values from -6 to 6
- grad_out: bfloat16 [2048, 4096], P('ep', 'tp'), may hold values from -6 to 6
- combine: bfloat16 [2048, 8], P('ep'), may hold values from 0.049804688 to 0.5
- expert_ids: int32 [2048, 8], P('ep'), may hold values from 0 to 63, all different within a row; in each aligned block of 32 rows (0 to 31, 32 to 63, ...) at most 5 rows name the same one
- w_gate: bfloat16 [64, 4096, 1536], P('ep', None, 'tp'), may hold values from -0.09375 to 0.09375
- w_up: bfloat16 [64, 4096, 1536], P('ep', None, 'tp'), may hold values from -0.09375 to 0.09375
- w_down: bfloat16 [64, 1536, 4096], P('ep', 'tp'), may hold values from -0.15625 to 0.15625
Outputs:
- d_tokens: bfloat16 [2048, 4096], P('ep', 'tp')
- d_combine: float32 [2048, 8], P('ep')
- grad_down: bfloat16 [64, 1536, 4096], P('ep', 'tp')
The draws below stay inside these ranges and needn't reach their ends.
Inputs may be any that keep to these rules, and one draw needn't show every extreme that they name: `expert_ids`: among the 32 tokens of one index of ep, no expert is named by more than 5 assignments, and some expert reaches 5; a token names 8 different experts.
All inputs are finite; a program needn't handle non-finite values.
Results may differ from the reference program's by a relative error of at most 0.025.
Values may be sent and summed in bfloat16 or wider, within the bound.
A program may use at most 32 MiB of HBM per device.

```python
import math
import jax
import jax.numpy as jnp
import numpy as np
from jax import lax

D = 4096
HID = 1536
TOP = 8
TOK_DEV = 32
EXPERTS = 64
CAP = 5
SLOTS = 320
TOKENS = 2048
N_EP = 64
N_TP = 16


def block_scale(rng, shape, split, smallest, top_value):
    def one(dim, shards_of):
        steps = jax.random.uniform(jax.random.fold_in(jax.random.fold_in(rng, 6), dim), (shards_of,), jnp.float32, smallest / len(split), top_value / len(split))
        return jnp.repeat(jnp.exp(steps), shape[dim] // shards_of).reshape((-1,) + (1,) * (len(shape) - dim - 1))

    gain = one(*split[0])
    for cut in split[1:]:
        gain = gain * one(*cut)
    return gain


def shared_out(rng, own, number, rows, number_of, top, reach, lean):
    sequence = jax.random.permutation(rng, number_of)
    packed, common = load_shares(number_of, rows * top, reach, lean, True), load_shares(number_of, rows * top, reach, lean, False)
    places = jnp.arange(number_of)

    def named(lengths, rotation):
        used = int((lengths > 0).sum())
        fixed = max(1, used // 4)
        passed = fixed + (places - fixed + rotation * (used - fixed)) % max(1, number_of - fixed)
        return jnp.zeros((number_of,), jnp.int32).at[sequence[jnp.where(places < fixed, places, passed)]].set(jnp.asarray(lengths, jnp.int32))

    lengths = jnp.where(number % 4 == 0, named(packed, number // 4), named(common, number - number // 4 - 1))
    mixed = jax.random.permutation(jax.random.fold_in(own, 3), number_of)
    donor, taker = mixed[0:number_of // 2 * 2:2], mixed[1:number_of // 2 * 2:2]
    slack = jnp.minimum(lengths[donor] - 1, reach - lengths[taker]) // 2
    slack = jnp.where((donor == sequence[0]) | (taker == sequence[0]) | (lengths[taker] == 0), 0, jnp.maximum(slack, 0))
    passed = jax.random.randint(jax.random.fold_in(own, 4), (number_of // 2,), 0, 1 << 20) % (slack + 1)
    lengths = lengths.at[donor].add(-passed).at[taker].add(passed)
    members = jnp.searchsorted(jnp.cumsum(lengths), jnp.arange(rows * top), side="right").astype(jnp.int32)
    grid = members.reshape(top, rows).T
    grid = grid[jax.random.permutation(jax.random.fold_in(own, 1), rows)]
    rotation = jax.random.randint(jax.random.fold_in(own, 2), (rows, 1), 0, top)
    return jnp.take_along_axis(grid, (jnp.arange(top)[None, :] + rotation) % top, axis=1)


def load_shares(number_of, total, reach, lean, full):
    weights = [(1 << 20) // math.isqrt(rank ** lean) + 1 for rank in range(1, number_of + 1)]
    largest = reach if full else min(reach, max(-(-total // number_of), total * weights[0] // sum(weights)))
    least = 1 if total - largest >= number_of - 1 else 0
    given, surplus = [largest] + [least] * (number_of - 1), total - largest - least * (number_of - 1)
    while surplus > 0:
        free = [i for i in range(1, number_of) if given[i] < largest] or [i for i in range(1, number_of) if given[i] < reach]
        mass, left = sum([weights[i] for i in free]), surplus
        for i in free:
            addition = min(reach - given[i], max(1, left * weights[i] // mass), surplus)
            given[i] = given[i] + addition
            surplus = surplus - addition
    return np.array(given)


def scatter_about(rng, dims, deviation, reach, shards=(), kind=jnp.bfloat16):
    values = jax.random.normal(rng, dims, jnp.float32) * deviation
    if len(shards) > 0:
        values = block_scale(rng, dims, shards, -0.22, 0.18) * values
    return jnp.clip(values, min=-reach, max=reach).astype(kind)


def setup_inputs(seed: int = 0) -> dict:
    arg_keys = jax.random.split(jax.random.key(seed), 8)
    tokens = scatter_about(arg_keys[0], (TOKENS, D), 1.0, 6.0, ((0, 64), (1, 16)))
    grad_out = scatter_about(arg_keys[1], (TOKENS, D), 1.0, 6.0, ((0, 64), (1, 16)))
    combine = jnp.clip(0.049804688 + 0.4501953 * jax.random.uniform(arg_keys[2], (TOKENS, TOP), jnp.float32) ** block_scale(arg_keys[2], (TOKENS, TOP), ((0, 64),), -0.2, 0.2), 0.049804688, 0.5).astype(jnp.bfloat16)
    expert_ids_keys = jax.random.split(jax.random.fold_in(arg_keys[3], 1), TOKENS // TOK_DEV)
    expert_ids_turns = jax.random.permutation(jax.random.fold_in(arg_keys[3], 3), TOKENS // TOK_DEV)
    expert_ids = jax.vmap(lambda own, number: shared_out(jax.random.fold_in(arg_keys[3], 2), own, number, TOK_DEV, EXPERTS, TOP, CAP, 2))(expert_ids_keys, expert_ids_turns).reshape((TOKENS, TOP))
    w_gate = scatter_about(arg_keys[4], (EXPERTS, D, HID), D ** -0.5, 0.09375, ((0, 64), (2, 16)))
    w_up = scatter_about(arg_keys[5], (EXPERTS, D, HID), D ** -0.5, 0.09375, ((0, 64), (2, 16)))
    w_down = scatter_about(arg_keys[6], (EXPERTS, HID, D), HID ** -0.5, 0.15625, ((0, 64), (1, 16)))
    return dict(tokens=tokens, grad_out=grad_out, combine=combine, expert_ids=expert_ids, w_gate=w_gate, w_up=w_up, w_down=w_down)


def reference(tokens, grad_out, combine, expert_ids, w_gate, w_up, w_down):
    flat_ids = expert_ids.reshape(-1).astype(jnp.int32)
    count = flat_ids.shape[0]
    expert_hot = (flat_ids[:, None] == jnp.arange(EXPERTS, dtype=jnp.int32)[None, :]).astype(jnp.int32)
    blocked = expert_hot.reshape(N_EP, TOK_DEV * TOP, EXPERTS)
    earlier = jnp.cumsum(blocked, axis=1) - blocked
    slot_index = jnp.sum(earlier * blocked, axis=2).reshape(-1).astype(jnp.int32)
    source = (jnp.arange(count, dtype=jnp.int32) // (TOK_DEV * TOP)).astype(jnp.int32)
    position = (flat_ids * SLOTS + source * CAP + slot_index).astype(jnp.int32)
    token_index = (jnp.arange(count, dtype=jnp.int32) // TOP).astype(jnp.int32)
    x_buffer = jnp.zeros((EXPERTS * SLOTS, D), tokens.dtype).at[position].set(tokens[token_index])
    dy_buffer = jnp.zeros((EXPERTS * SLOTS, D), grad_out.dtype).at[position].set(grad_out[token_index])
    w_buffer = jnp.zeros((EXPERTS * SLOTS,), combine.dtype).at[position].set(combine.reshape(-1))
    group_units = HID // N_TP

    def per_expert(items):
        x_rows, dy_rows, w_rows, gate_matrix, up_matrix, down_matrix = items
        gate_pre = jnp.dot(x_rows, gate_matrix, preferred_element_type=jnp.float32)
        up_pre = jnp.dot(x_rows, up_matrix, preferred_element_type=jnp.float32)
        hidden_grad = jnp.dot(dy_rows, down_matrix.T, preferred_element_type=jnp.float32)
        weight_col = w_rows.astype(jnp.float32)[:, None]
        activation = jax.nn.silu(gate_pre)
        product = activation * up_pre
        hidden = product.astype(jnp.bfloat16)
        weighted = (weight_col * product).astype(jnp.bfloat16)
        scaled = weight_col * hidden_grad
        up_grad = (scaled * activation).astype(jnp.bfloat16)
        sigma = jax.nn.sigmoid(gate_pre)
        gate_grad = (scaled * up_pre * sigma * (1.0 + gate_pre * (1.0 - sigma))).astype(jnp.bfloat16)
        gate_groups = gate_grad.astype(jnp.float32).reshape(SLOTS, N_TP, group_units)
        up_groups = up_grad.astype(jnp.float32).reshape(SLOTS, N_TP, group_units)
        gate_w = gate_matrix.astype(jnp.float32).reshape(D, N_TP, group_units)
        up_w = up_matrix.astype(jnp.float32).reshape(D, N_TP, group_units)
        input_part = jnp.einsum("rgh,dgh->grd", gate_groups, gate_w) + jnp.einsum("rgh,dgh->grd", up_groups, up_w)
        input_part = input_part.astype(jnp.bfloat16).astype(jnp.float32)
        slot_input = jnp.sum(input_part, axis=0).astype(jnp.bfloat16)
        comb_groups = jnp.sum((hidden.astype(jnp.float32) * hidden_grad).reshape(SLOTS, N_TP, group_units), axis=2)
        slot_comb = jnp.sum(comb_groups.astype(jnp.bfloat16).astype(jnp.float32), axis=1)
        down_grad = jnp.dot(weighted.T, dy_rows, preferred_element_type=jnp.float32).astype(jnp.bfloat16)
        return slot_input, slot_comb, down_grad

    results = lax.map(per_expert, (x_buffer.reshape(EXPERTS, SLOTS, D), dy_buffer.reshape(EXPERTS, SLOTS, D),
                                   w_buffer.reshape(EXPERTS, SLOTS), w_gate, w_up, w_down))
    input_all = results[0].reshape(EXPERTS * SLOTS, D)[position].reshape(TOKENS, TOP, D)
    d_tokens = jnp.sum(input_all.astype(jnp.float32), axis=1).astype(jnp.bfloat16)
    d_combine = results[1].reshape(-1)[position].reshape(TOKENS, TOP)
    return d_tokens, d_combine, results[2]
```

```python
import functools

import jax
import jax.numpy as jnp
from jax import lax
from jax.experimental import pallas as pl
from jax.experimental.pallas import tpu as pltpu
from jax.sharding import PartitionSpec as P

MESH = pl.DeviceIdType.MESH
F32 = jnp.float32
BF16 = jnp.bfloat16
CAP = 5
GROUP = 16
NN = (((1,), (0,)), ((), ()))
NT = (((1,), (1,)), ((), ()))
TN = (((0,), (0,)), ((), ()))


def dot(a, b, dims=NN, precision=None):
    return lax.dot_general(a, b, dims, preferred_element_type=F32, precision=precision)


def iota(shape, dim):
    return lax.broadcasted_iota(jnp.int32, shape, dim)


def packed_row(i):
    part = (i >= 80).astype(jnp.int32) + (i >= 160).astype(jnp.int32)
    j = i - part * 80
    s = (j * 205) >> 10
    c = j - s * 5
    scalar = s * 16 + c + 5 + jnp.where(c >= 3, 5, 0)
    return jnp.where(part == 2, scalar, s * 16 + part * 8 + c)


def kernel(
    n_ep,
    n_tp,
    ids,
    comb,
    tok,
    gout,
    wg,
    wu,
    wd,
    dtok,
    dcomb,
    gdown,
    w2,
    wdp,
    ohx,
    ohw,
    sx,
    sdy,
    rx,
    rdy,
    fx,
    fdy,
    acc,
    acch,
    wcol,
    bg,
    wt,
    cb,
    pown,
    pout,
    pin,
    sbuf,
    arr_r,
    arr_l,
    sback,
    rback,
    gd,
    w_sem,
    ep_s,
    ep_r,
    ag_rs,
    ag_rr,
    ag_ls,
    ag_lr,
    sib_s,
    sib_r,
    pair_s,
    pair_r,
    rs_rs,
    rs_rr,
    rs_ls,
    rs_lr,
    cb_s,
    cb_r,
    gd_sem,
):
    nz = n_tp // 2
    ep = lax.axis_index("ep")
    tp = lax.axis_index("tp")
    z = lax.div(tp, 2)
    c = lax.rem(tp, 2)
    right = lax.rem(z + 1, nz) * 2 + c
    left = lax.rem(z + nz - 1, nz) * 2 + c
    sib = z * 2 + 1 - c
    slots = fx.shape[1]
    feat = fx.shape[2]
    half_rows = slots // 2
    hid = wg.shape[0]
    groups = n_ep // GROUP

    def rcopy(src, dst, s, r, axis, to):
        return pltpu.make_async_remote_copy(
            src_ref=src, dst_ref=dst, send_sem=s, recv_sem=r, device_id={axis: to}, device_id_type=MESH
        )

    loads = (
        pltpu.make_async_copy(wg, w2.at[pl.ds(0, hid)], w_sem.at[0]),
        pltpu.make_async_copy(wu, w2.at[pl.ds(128, hid)], w_sem.at[1]),
        pltpu.make_async_copy(wd, wdp.at[pl.ds(0, hid)], w_sem.at[2]),
    )
    for load in loads:
        load.start()

    barrier = pltpu.get_barrier_semaphore()

    def greet_ep(i, _):
        pl.semaphore_signal(barrier, inc=1, device_id={"ep": lax.rem(ep + i, n_ep)}, device_id_type=MESH)
        return 0

    def greet_tp(i, _):
        pl.semaphore_signal(barrier, inc=1, device_id={"tp": lax.rem(tp + i, n_tp)}, device_id_type=MESH)
        return 0

    lax.fori_loop(1, n_ep, greet_ep, 0)
    lax.fori_loop(1, n_tp, greet_tp, 0)

    tokens = tok.shape[0]
    expert = iota((n_ep, tokens), 0)
    named = jnp.zeros((n_ep, tokens), F32)
    weight = jnp.zeros((n_ep, tokens), F32)
    for k in range(ids.shape[0]):
        hit = ids[k : k + 1, :] == expert
        named = jnp.where(hit, 1.0, named)
        weight = jnp.where(hit, comb[k : k + 1, :].astype(F32), weight)
    earlier = (iota((tokens, tokens), 0) < iota((tokens, tokens), 1)).astype(F32).astype(BF16)
    rank = dot(named.astype(BF16), earlier)
    code = jnp.where(named > 0.5, rank, 99.0).astype(BF16)
    weight = weight.astype(BF16)
    for g in range(groups):
        row = iota((256, n_ep), 0) + 256 * g
        spread = ((row >> 4) == iota((256, n_ep), 1)).astype(F32).astype(BF16)
        code_rows = dot(spread, code)
        weight_rows = dot(spread, weight)
        r = iota((256, tokens), 0)
        cc = r & 7
        wanted = jnp.where(cc < CAP, cc, cc - CAP + 3 * ((r >> 3) & 1)).astype(F32)
        hot = (code_rows == wanted).astype(F32)
        rows = pl.ds(256 * g, 256)
        ohx[rows, :] = jnp.where(cc < CAP, hot, 0.0).astype(BF16)
        ohw[rows, :] = jnp.where(cc < CAP, 0.0, hot).astype(BF16)
        scalar = dot((jnp.where(cc < CAP, 0.0, hot) * weight_rows).astype(BF16), jnp.ones((tokens, 128), BF16))
        both = dot(ohx[rows, :], tok[...])
        upper = (iota((256, 128), 0) & 8) == 0
        block = jnp.where(upper, both[:, :128], both[:, 128:]) + scalar
        sx[pl.ds(GROUP * g, GROUP)] = block.astype(BF16).reshape(GROUP, 16, 128)

    pl.semaphore_wait(barrier, n_ep - 1 + n_tp - 1)

    def send_blocks(src, dst, index):
        def one(i, _):
            to = lax.rem(ep + i, n_ep)
            rcopy(src.at[to], dst.at[ep], ep_s.at[index], ep_r.at[index], "ep", to).start()
            return 0

        lax.fori_loop(1, n_ep, one, 0)
        dst[pl.ds(ep, 1)] = src[pl.ds(ep, 1)]

    def all_blocks(src, dst, index):
        some = pl.ds(0, n_ep - 1)
        return rcopy(src.at[some], dst.at[some], ep_s.at[index], ep_r.at[index], "ep", lax.rem(ep + 1, n_ep))

    send_blocks(sx, rx, 0)
    for g in range(groups):
        rows = pl.ds(256 * g, 256)
        both = dot(ohx[rows, :], gout[...])
        upper = (iota((256, 128), 0) & 8) == 0
        block = jnp.where(upper, both[:, :128], both[:, 128:])
        sdy[pl.ds(GROUP * g, GROUP)] = block.astype(BF16).reshape(GROUP, 16, 128)
    send_blocks(sdy, rdy, 1)

    gap = 128 - hid
    blank = jnp.zeros((gap, w2.shape[1]), BF16)
    w2[pl.ds(hid, gap), :] = blank
    w2[pl.ds(128 + hid, gap), :] = blank
    wdp[pl.ds(hid, gap), :] = blank
    acc[...] = jnp.zeros_like(acc)
    acch[...] = jnp.zeros_like(acch)
    cb[pl.ds(tp, 1)] = jnp.zeros((1, 8, 128), F32)
    for load in loads:
        load.wait()
    pick = (iota((240, 256), 1) == packed_row(iota((240, 256), 0))).astype(F32).astype(BF16)

    full = (fx, fdy)
    got = (rx, rdy)
    sent = (sx, sdy)

    def half(ref, h):
        return ref.at[pl.ds(h * half_rows, half_rows)]

    def chunk(k, own):
        return lax.rem(z + k + nz, nz) * 2 + (c if own else 1 - c)

    def to_right(t, j, h, q):
        piece = half(full[t].at[q], h)
        return rcopy(piece, piece, ag_rs.at[t, j, h], ag_rr.at[t, j, h], "tp", right)

    def to_left(t, j, h, q):
        piece = half(full[t].at[q], h)
        return rcopy(piece, piece, ag_ls.at[t, j, h], ag_lr.at[t, j, h], "tp", left)

    def to_sib(t, i, q):
        piece = full[t].at[q]
        return rcopy(piece, piece, sib_s.at[t, i], sib_r.at[t, i], "tp", sib)

    def consume(t, q):
        columns = pl.ds(pl.multiple_of(q * feat, feat), feat)
        if t == 0:
            acc[...] += dot(fx[q], w2[:, columns], NT)
        else:
            acch[...] += dot(fdy[q], wdp[:, columns], NT)

    def consume_pair(t, j, own):
        def one(i, _):
            consume(t, chunk(j * (2 * i - 1), own))
            return 0

        lax.fori_loop(0, 2, one, 0)

    mine = chunk(0, True)
    for t in range(2):
        all_blocks(sent[t], got[t], t).wait_recv()
        for g in range(groups):
            block = got[t][pl.ds(GROUP * g, GROUP)].reshape(256, 128)
            packed = dot(pick if t == 0 else pick[:160], block)
            rows = pl.ds(80 * g, 80)
            full[t][tp, rows, :128] = packed[:80].astype(BF16)
            full[t][tp, rows, 128:] = packed[80:160].astype(BF16)
            if t == 0:
                wcol[rows, :] = packed[160:]
        to_right(t, 0, 0, mine).start()
        to_left(t, 0, 1, mine).start()
        to_right(t, 0, 1, mine).start()
        to_left(t, 0, 0, mine).start()
        to_sib(t, 0, mine).start()
    consume(0, mine)
    consume(1, mine)
    for t in range(2):
        to_sib(t, 0, chunk(0, False)).wait_recv()
        consume(t, chunk(0, False))

    def stage(j, _):
        for t in range(2):
            from_left, from_right = chunk(-j, True), chunk(j, True)
            to_right(t, j - 1, 0, from_left).wait_recv()
            to_right(t, j, 0, from_left).start()
            to_left(t, j - 1, 1, from_right).wait_recv()
            to_left(t, j, 1, from_right).start()
            to_right(t, j - 1, 1, from_left).wait_recv()

            @pl.when(j < nz // 2 - 1)
            def _():
                to_right(t, j, 1, from_left).start()

            to_left(t, j - 1, 0, from_right).wait_recv()

            @pl.when(j < nz // 2 - 1)
            def _():
                to_left(t, j, 0, from_right).start()

            to_sib(t, j, from_left).start()
            to_sib(t, nz // 2 + j, from_right).start()
            consume_pair(t, j, True)
        for t in range(2):
            to_sib(t, j, chunk(-j, False)).wait_recv()
            to_sib(t, nz // 2 + j, chunk(j, False)).wait_recv()
            consume_pair(t, j, False)
        return 0

    last = nz // 2
    lax.fori_loop(1, last, stage, 0)
    for t in range(2):
        q = chunk(last, True)
        to_right(t, last - 1, 0, q).wait_recv()
        to_left(t, last - 1, 1, q).wait_recv()
        to_sib(t, last, q).start()
        consume(t, q)
    for t in range(2):
        q = chunk(last, False)
        to_sib(t, last, q).wait_recv()
        consume(t, q)

    for g in range(groups):
        rows = pl.ds(80 * g, 80)
        gate, up, back = acc[rows, :128], acc[rows, 128:], acch[rows, :]
        w = wcol[rows, :]
        sigma = jax.nn.sigmoid(gate)
        act = gate * sigma
        product = act * up
        hidden = product.astype(BF16).astype(F32)
        wt[rows, :] = (w * product).astype(BF16)
        scaled = w * back
        bg[rows, :128] = (scaled * up * sigma * (1.0 + gate * (1.0 - sigma))).astype(BF16)
        bg[rows, 128:] = (scaled * act).astype(BF16)
        line = dot(jnp.ones((8, 128), F32), hidden * back, NT, lax.Precision.HIGHEST)
        cb[tp, g : g + 1, :80] = line[:1]

    def pair(k):
        return rcopy(pout.at[k], pin.at[k], pair_s.at[k], pair_r.at[k], "tp", sib)

    def calc(k):
        def part(q):
            columns = pl.ds(pl.multiple_of(q * feat, feat), feat)
            return dot(bg[...], w2[:, columns]).astype(BF16)

        pout[k] = part(chunk(k, False))
        pair(k).start()
        pown[k] = part(chunk(k, True))

    def calc_pair(k):
        def one(i, _):
            calc(k + i * (nz - 2 * k))
            return 0

        lax.fori_loop(0, 2, one, 0)

    def put(k, h, arrived):
        rows = pl.ds(h * half_rows, half_rows)
        value = pown[k, rows, :].astype(F32) + pin[k, rows, :].astype(F32)
        if arrived is not None:
            value = value + arrived[rows, :].astype(F32)
        sbuf[k, rows, :] = value.astype(BF16)

    def sum_right(k, h):
        return rcopy(
            half(sbuf.at[k], h), half(arr_r.at[k - 1], h), rs_rs.at[k - 1, h], rs_rr.at[k - 1, h], "tp", right
        )

    def sum_left(k, h):
        return rcopy(
            half(sbuf.at[nz - k], h), half(arr_l.at[k - 1], h), rs_ls.at[k - 1, h], rs_lr.at[k - 1, h], "tp", left
        )

    calc(last)
    calc_pair(last - 1)

    def tell(i, _):
        rcopy(cb.at[tp], cb.at[tp], cb_s, cb_r, "tp", lax.rem(tp + i, n_tp)).start()
        return 0

    lax.fori_loop(1, n_tp, tell, 0)
    pair(last).wait_recv()
    put(last, 0, None)
    sum_right(last, 0).start()
    put(last, 1, None)
    sum_left(last, 1).start()
    for k in range(last - 1, 0, -1):
        first = k == last - 1
        pair(k).wait_recv()
        if not first:
            sum_right(k + 1, 1).wait_recv()
        put(k, 1, None if first else arr_r.at[k])
        sum_right(k, 1).start()
        pair(nz - k).wait_recv()
        if not first:
            sum_left(k + 1, 0).wait_recv()
        put(nz - k, 0, None if first else arr_l.at[k])
        sum_left(k, 0).start()
        if k > 1:
            calc_pair(k - 1)
        else:
            calc(0)
        sum_right(k + 1, 0).wait_recv()
        put(k, 0, arr_r.at[k])
        sum_right(k, 0).start()
        sum_left(k + 1, 1).wait_recv()
        put(nz - k, 1, arr_l.at[k])
        sum_left(k, 1).start()

    some = pl.ds(0, n_tp - 1)
    comb_all = rcopy(cb.at[some], cb.at[some], cb_s, cb_r, "tp", right)
    comb_all.wait_recv()
    comb_sum = jnp.sum(cb[...], axis=0)
    place = (iota((256, 160), 0) == packed_row(iota((256, 160), 1))).astype(F32).astype(BF16)
    place_scalar = (iota((256, 80), 0) == packed_row(iota((256, 80), 1) + 160)).astype(F32)
    pair(0).wait_recv()
    for h in (1, 0):
        sum_right(1, h).wait_recv()
        sum_left(1, h).wait_recv()
    for g in range(groups):
        rows = pl.ds(80 * g, 80)
        total = pown[0, rows, :].astype(F32) + pin[0, rows, :].astype(F32)
        total = total + arr_r[0, rows, :].astype(F32) + arr_l[0, rows, :].astype(F32)
        total = total.astype(BF16)
        packed = jnp.concatenate([total[:, :128], total[:, 128:]], axis=0)
        line = (place_scalar * comb_sum[g : g + 1, :80]).astype(BF16)
        block = dot(place, packed) + dot(line, jnp.ones((80, 128), BF16))
        sback[pl.ds(GROUP * g, GROUP)] = block.astype(BF16).reshape(GROUP, 16, 128)
    send_blocks(sback, rback, 2)

    def down(q, _):
        columns = pl.ds(pl.multiple_of(q * feat, feat), feat)
        gd[:, columns] = dot(wt[...], fdy[q], TN)[:hid].astype(BF16)
        return 0

    lax.fori_loop(0, n_tp, down, 0)
    out = pltpu.make_async_copy(gd, gdown, gd_sem)
    out.start()

    all_blocks(sback, rback, 2).wait_recv()
    back = rback[...].reshape(n_ep * 16, 128)
    hot = ohx[...]
    upper = (iota((n_ep * 16, tokens), 0) & 8) == 0
    zero = jnp.zeros_like(hot)
    dtok[:, :128] = dot(jnp.where(upper, hot, zero), back, TN).astype(BF16)
    dtok[:, 128:] = dot(jnp.where(upper, zero, hot), back, TN).astype(BF16)
    chosen = ohw[...] * back[:, :tokens]
    gather = ((iota((n_ep, n_ep * 16), 1) >> 4) == iota((n_ep, n_ep * 16), 0)).astype(F32).astype(BF16)
    by_expert = dot(gather, chosen)
    for k in range(ids.shape[0]):
        hit = ids[k : k + 1, :] == expert
        dcomb[k : k + 1, :] = jnp.sum(jnp.where(hit, by_expert, 0.0), axis=0, keepdims=True)

    for t in range(2):
        all_blocks(sent[t], got[t], t).wait_send()
        for j in range(last):
            for h in range(2):
                if j < last - 1 or h == 0:
                    to_right(t, j, h, mine).wait_send()
                if j < last - 1 or h == 1:
                    to_left(t, j, h, mine).wait_send()
        for i in range(nz):
            to_sib(t, i, mine).wait_send()
    all_blocks(sback, rback, 2).wait_send()
    comb_all.wait_send()
    for k in range(nz):
        pair(k).wait_send()
    for k in range(1, last + 1):
        for h in range(2):
            if k < last or h == 0:
                sum_right(k, h).wait_send()
            if k < last or h == 1:
                sum_left(k, h).wait_send()
    out.wait()


def per_device(n_ep, n_tp, tokens, grad_out, combine, expert_ids, w_gate, w_up, w_down):
    tok_count, feat = tokens.shape
    top = expert_ids.shape[1]
    hid, width = w_down.shape[1:]
    slots = n_ep * CAP
    nz = n_tp // 2
    vmem = pl.BlockSpec(memory_space=pltpu.VMEM)
    anyw = pl.BlockSpec(memory_space=pl.ANY)
    dma = pltpu.SemaphoreType.DMA
    blocks = pltpu.VMEM((n_ep, 16, 128), BF16)
    chunks = pltpu.VMEM((n_tp, slots, feat), BF16)
    parts = pltpu.VMEM((nz, slots, feat), BF16)
    d_tokens, d_combine, down = pl.pallas_call(
        functools.partial(kernel, n_ep, n_tp),
        out_shape=(
            jax.ShapeDtypeStruct((tok_count, feat), BF16),
            jax.ShapeDtypeStruct((top, tok_count), F32),
            jax.ShapeDtypeStruct((hid, width), BF16),
        ),
        in_specs=[vmem, vmem, vmem, vmem, anyw, anyw, anyw],
        out_specs=(vmem, vmem, anyw),
        scratch_shapes=[
            pltpu.VMEM((256, width), BF16),
            pltpu.VMEM((128, width), BF16),
            pltpu.VMEM((n_ep * 16, tok_count), BF16),
            pltpu.VMEM((n_ep * 16, tok_count), BF16),
            blocks,
            blocks,
            blocks,
            blocks,
            chunks,
            chunks,
            pltpu.VMEM((slots, 256), F32),
            pltpu.VMEM((slots, 128), F32),
            pltpu.VMEM((slots, 128), F32),
            pltpu.VMEM((slots, 256), BF16),
            pltpu.VMEM((slots, 128), BF16),
            pltpu.VMEM((n_tp, 8, 128), F32),
            parts,
            parts,
            parts,
            parts,
            pltpu.VMEM((nz // 2, slots, feat), BF16),
            pltpu.VMEM((nz // 2, slots, feat), BF16),
            blocks,
            blocks,
            pltpu.VMEM((hid, width), BF16),
            dma((3,)),
            dma((3,)),
            dma((3,)),
            dma((2, nz // 2, 2)),
            dma((2, nz // 2, 2)),
            dma((2, nz // 2, 2)),
            dma((2, nz // 2, 2)),
            dma((2, nz)),
            dma((2, nz)),
            dma((nz,)),
            dma((nz,)),
            dma((nz // 2, 2)),
            dma((nz // 2, 2)),
            dma((nz // 2, 2)),
            dma((nz // 2, 2)),
            dma,
            dma,
            dma,
        ],
        compiler_params=pltpu.CompilerParams(
            collective_id=0, has_side_effects=True, vmem_limit_bytes=48 * 1024 * 1024
        ),
    )(expert_ids.T, combine.T, tokens, grad_out, w_gate[0].T, w_up[0].T, w_down[0])
    return d_tokens, d_combine.T, down[None]


def solution(mesh):
    placed = (
        P("ep", "tp"),
        P("ep", "tp"),
        P("ep", None),
        P("ep", None),
        P("ep", None, "tp"),
        P("ep", None, "tp"),
        P("ep", "tp", None),
    )
    return jax.shard_map(
        functools.partial(per_device, mesh.shape["ep"], mesh.shape["tp"]),
        mesh=mesh,
        in_specs=placed,
        out_specs=(P("ep", "tp"), P("ep", None), P("ep", "tp", None)),
        check_vma=False,
    )
```

```python
import functools
import math

import jax
import jax.numpy as jnp
from jax import lax
from jax.experimental import pallas as pl
from jax.experimental.pallas import tpu as pltpu
from jax.sharding import PartitionSpec as P

MESH = pl.DeviceIdType.MESH
F32 = jnp.float32
BF16 = jnp.bfloat16
CAP = 5
ROWS = 6
NN = (((1,), (0,)), ((), ()))
NT = (((1,), (1,)), ((), ()))
TN = (((0,), (0,)), ((), ()))


def dot(a, b, dims=NN, precision=None):
    return lax.dot_general(a, b, dims, preferred_element_type=F32, precision=precision)


def iota(shape, dim):
    return lax.broadcasted_iota(jnp.int32, shape, dim)


def where_block(u, swapped, side):
    return (u & (side - 1)) * side + lax.div(u, side) if swapped else u


def slot_of(i):
    s = (i * 3277) >> 14
    return s, i - s * CAP


def block_of(r):
    u = (r * 10923) >> 16
    return u, r - u * ROWS


def ones_where(mask):
    return jnp.where(mask, 1.0, 0.0).astype(BF16)


def kernel(
    n_ep,
    n_tp,
    ids,
    comb,
    tok_hbm,
    gout_hbm,
    wg,
    wu,
    wd,
    dtok,
    dcomb,
    gdown,
    tok,
    gout,
    far,
    w2,
    wdp,
    hot,
    code,
    picks,
    places,
    s1,
    r1,
    s2,
    r2,
    fx,
    fdy,
    acc,
    acch,
    wcol,
    bg,
    wt,
    cb,
    pown,
    pout,
    pin,
    sbuf,
    arr_r,
    arr_l,
    gd,
    w_sem,
    ep_s,
    ep_r,
    ag_rs,
    ag_rr,
    ag_ls,
    ag_lr,
    sib_s,
    sib_r,
    pair_s,
    pair_r,
    rs_rs,
    rs_rr,
    rs_ls,
    rs_lr,
    cb_s,
    cb_r,
    gd_sem,
    far_s,
    far_r,
):
    side = s1.shape[2]
    nz = n_tp // 2
    ep = lax.axis_index("ep")
    tp = lax.axis_index("tp")
    gx = lax.div(ep, side)
    gy = lax.rem(ep, side)
    z = lax.div(tp, 2)
    c = lax.rem(tp, 2)
    right = lax.rem(z + 1, nz) * 2 + c
    left = lax.rem(z + nz - 1, nz) * 2 + c
    sib = z * 2 + 1 - c
    opposite = lax.rem(z + nz // 2, nz) * 2 + c
    slots = fx.shape[1]
    feat = fx.shape[2]
    half_rows = slots // 2
    hid = wg.shape[0]
    lines = n_ep * ROWS

    def rcopy(src, dst, s, r, axis, to):
        return pltpu.make_async_remote_copy(
            src_ref=src, dst_ref=dst, send_sem=s, recv_sem=r, device_id={axis: to}, device_id_type=MESH
        )

    def neighbour(i, along_y):
        if along_y:
            return gx * side + lax.rem(gy + i, side)
        return lax.rem(gx + i, side) * side + gy

    loads = (
        pltpu.make_async_copy(tok_hbm, tok, w_sem.at[0]),
        pltpu.make_async_copy(gout_hbm, gout, w_sem.at[1]),
        pltpu.make_async_copy(wg, w2.at[pl.ds(0, hid)], w_sem.at[2]),
        pltpu.make_async_copy(wu, w2.at[pl.ds(128, hid)], w_sem.at[3]),
        pltpu.make_async_copy(wd, wdp.at[pl.ds(0, hid)], w_sem.at[4]),
    )
    for load in loads:
        load.start()

    barrier = pltpu.get_barrier_semaphore()

    def greet_y(i, _):
        pl.semaphore_signal(barrier, inc=1, device_id={"ep": neighbour(i, True)}, device_id_type=MESH)
        return 0

    def greet_x(i, _):
        pl.semaphore_signal(barrier, inc=1, device_id={"ep": neighbour(i, False)}, device_id_type=MESH)
        return 0

    def greet_tp(i, _):
        pl.semaphore_signal(barrier, inc=1, device_id={"tp": lax.rem(tp + i, n_tp)}, device_id_type=MESH)
        return 0

    lax.fori_loop(1, side, greet_y, 0)
    lax.fori_loop(1, side, greet_x, 0)
    lax.fori_loop(1, n_tp, greet_tp, 0)

    tokens = tok.shape[0]
    expert = iota((n_ep, tokens), 0)
    named = jnp.zeros((n_ep, tokens), F32)
    weight = jnp.zeros((n_ep, tokens), F32)
    for k in range(ids.shape[0]):
        hit = ids[k : k + 1, :] == expert
        named = jnp.where(hit, 1.0, named)
        weight = jnp.where(hit, comb[k : k + 1, :].astype(F32), weight)
    earlier = ones_where(iota((tokens, tokens), 0) < iota((tokens, tokens), 1))
    rank = dot(named.astype(BF16), earlier)
    code[...] = jnp.where(named > 0.5, rank, 99.0)
    lane = iota((n_ep, 128), 1)
    scalars = jnp.zeros((n_ep, 128), F32)
    for k in range(CAP):
        one = jnp.sum(jnp.where(code[...] == k, weight, 0.0), axis=1, keepdims=True)
        scalars = jnp.where(lane == k, one, scalars)
    block, line = block_of(iota((lines, n_ep), 0))
    _, line_t = block_of(iota((lines, tokens), 0))
    for h in range(2):
        spread = where_block(block, h == 0, side) == iota((lines, n_ep), 1)
        rows = dot(ones_where(spread), code[...].astype(BF16))
        hot[h] = ones_where(rows == line_t.astype(F32))
        if h == 0:
            extra = dot(ones_where(spread & (line == CAP)), scalars.astype(BF16))

    def lay(t, tokens_of, more):
        for h in range(2):
            laid = dot(hot[h], tokens_of[:, 128 * h : 128 * h + 128])
            if h == 0 and more is not None:
                laid = laid + more
            s1[t, h] = laid.astype(BF16).reshape(side, side * ROWS, 128)

    loads[0].wait()
    lay(0, tok, extra)

    pl.semaphore_wait(barrier, 2 * (side - 1) + n_tp - 1)

    out_of, into = (s1, s2), (r1, r2)

    def swap(t, h, phase):
        along_y = (h == 0) == (phase == 0)
        me = gy if along_y else gx
        src, dst = out_of[phase], into[phase]

        def one(i, _):
            to = lax.rem(me + i, side)
            rcopy(
                src.at[t, h, to],
                dst.at[t, h, me],
                ep_s.at[t, h, phase],
                ep_r.at[t, h, phase],
                "ep",
                neighbour(i, along_y),
            ).start()
            return 0

        lax.fori_loop(1, side, one, 0)
        dst[t, h, pl.ds(me, 1)] = src[t, h, pl.ds(me, 1)]

    def swapped(t, h, phase):
        some = pl.ds(0, side - 1)
        return rcopy(
            out_of[phase].at[t, h, some],
            into[phase].at[t, h, some],
            ep_s.at[t, h, phase],
            ep_r.at[t, h, phase],
            "ep",
            neighbour(1, (h == 0) == (phase == 0)),
        )

    def to_opposite(t):
        return rcopy((tok, gout)[t], far.at[t], far_s.at[t], far_r.at[t], "tp", opposite)

    swap(0, 0, 0)
    swap(0, 1, 0)
    loads[1].wait()
    lay(1, gout, None)
    swap(1, 0, 0)
    swap(1, 1, 0)
    to_opposite(0).start()
    to_opposite(1).start()

    gap = 128 - hid
    blank = jnp.zeros((gap, w2.shape[1]), BF16)
    w2[pl.ds(hid, gap), :] = blank
    w2[pl.ds(128 + hid, gap), :] = blank
    wdp[pl.ds(hid, gap), :] = blank
    acc[...] = jnp.zeros_like(acc)
    acch[...] = jnp.zeros_like(acch)
    block, line = block_of(iota((lines, lines), 0))
    turn = ones_where(where_block(block, True, side) * ROWS + line == iota((lines, lines), 1))

    source, slot = slot_of(iota((slots, lines), 0))
    column = iota((slots, lines), 1)
    picks[0] = ones_where(source * ROWS + slot == column)
    picks[1] = ones_where(where_block(source, True, side) * ROWS + slot == column)
    picks[2] = ones_where(source * ROWS + CAP == column)

    def forward(t, h):
        swapped(t, h, 0).wait_recv()
        turned = dot(turn, r1[t, h].reshape(lines, 128))
        s2[t, h] = turned.astype(BF16).reshape(side, side * ROWS, 128)
        swap(t, h, 1)

    for t in range(2):
        for h in range(2):
            forward(t, h)
    for load in loads[2:]:
        load.wait()

    full = (fx, fdy)
    last = nz // 2

    def half(ref, h):
        return ref.at[pl.ds(h * half_rows, half_rows)]

    def chunk(k, own):
        return lax.rem(z + k + nz, nz) * 2 + (c if own else 1 - c)

    def to_right(t, j, h, q):
        piece = half(full[t].at[q], h)
        return rcopy(piece, piece, ag_rs.at[t, j, h], ag_rr.at[t, j, h], "tp", right)

    def to_left(t, j, h, q):
        piece = half(full[t].at[q], h)
        return rcopy(piece, piece, ag_ls.at[t, j, h], ag_lr.at[t, j, h], "tp", left)

    def to_sib(t, i, q):
        piece = full[t].at[q]
        return rcopy(piece, piece, sib_s.at[t, i], sib_r.at[t, i], "tp", sib)

    def consume(t, q):
        columns = pl.ds(pl.multiple_of(q * feat, feat), feat)
        if t == 0:
            acc[...] += dot(fx[q], w2[:, columns], NT)
        else:
            acch[...] += dot(fdy[q], wdp[:, columns], NT)

    def consume_pair(t, j, own):
        def one(i, _):
            consume(t, chunk(j * (2 * i - 1), own))
            return 0

        lax.fori_loop(0, 2, one, 0)

    mine = chunk(0, True)

    def unpack(t, blocks, q):
        for h in range(2):
            swapped(blocks, h, 1).wait_recv()
            packed = dot(picks[h], r2[blocks, h].reshape(lines, 128))
            full[t][q, :, 128 * h : 128 * h + 128] = packed.astype(BF16)

    def own_chunk(t):
        unpack(t, t, mine)
        to_right(t, 0, 0, mine).start()
        to_left(t, 0, 1, mine).start()
        to_right(t, 0, 1, mine).start()
        to_left(t, 0, 0, mine).start()
        to_sib(t, 0, mine).start()
        consume(t, mine)

    def arrival(t, j):
        from_left, from_right = chunk(-j, True), chunk(j, True)
        for h in range(2):
            to_right(t, j - 1, h, from_left).wait_recv()
            if j < last - 1:
                to_right(t, j, h, from_left).start()
            to_left(t, j - 1, 1 - h, from_right).wait_recv()
            if j < last - 1:
                to_left(t, j, 1 - h, from_right).start()
        to_sib(t, j, from_left).start()
        to_sib(t, last + j, from_right).start()
        consume_pair(t, j, True)

    def from_sib(t, j):
        to_sib(t, j, chunk(-j, False)).wait_recv()
        if 0 < j < last:
            to_sib(t, last + j, chunk(j, False)).wait_recv()
            consume_pair(t, j, False)
        else:
            consume(t, chunk(j, False))

    def farthest(t):
        q = chunk(last, True)
        unpack(t, 3 + t, q)
        to_sib(t, last, q).start()
        consume(t, q)

    own_chunk(0)
    own_chunk(1)
    picked = dot(picks[2], r2[0, 0].reshape(lines, 128))
    _, slot_here = slot_of(iota((slots, 128), 0))
    picked = jnp.where(iota((slots, 128), 1) == slot_here, picked, 0.0).astype(BF16)
    wcol[...] = dot(picked, jnp.ones((128, 128), BF16))
    for t in range(2):
        to_opposite(t).wait_recv()
        lay(3 + t, far.at[t], None)
        swap(3 + t, 0, 0)
        swap(3 + t, 1, 0)
    for t in range(2):
        arrival(t, 1)
    for t in range(2):
        for h in range(2):
            forward(3 + t, h)
    for t in range(2):
        from_sib(t, 0)
        from_sib(t, 1)
    for t in range(2):
        arrival(t, 2)
    source, slot = slot_of(iota((lines, slots), 1))
    row = iota((lines, slots), 0)
    major = where_block(source, True, side) * ROWS
    places[0] = ones_where(row == major + slot)
    places[1] = ones_where(row == source * ROWS + slot)
    places[2] = ones_where(row == major + CAP)
    for t in range(2):
        farthest(t)
        from_sib(t, 2)
    for t in range(2):
        arrival(t, 3)
    for t in range(2):
        from_sib(t, last)
        from_sib(t, 3)

    for g in range(slots // 80):
        rows = pl.ds(80 * g, 80)
        gate, up, back = acc[rows, :128], acc[rows, 128:], acch[rows, :]
        w = wcol[rows, :]
        sigma = jax.nn.sigmoid(gate)
        act = gate * sigma
        product = act * up
        scaled = w * back
        bg[rows, :128] = (scaled * up * sigma * (1.0 + gate * (1.0 - sigma))).astype(BF16)
        bg[rows, 128:] = (scaled * act).astype(BF16)
        acch[rows, :] = product.astype(BF16).astype(F32) * back
        wcol[rows, :] = w * product

    def pair(k):
        return rcopy(pout.at[k], pin.at[k], pair_s.at[k], pair_r.at[k], "tp", sib)

    def calc(k):
        def part(q):
            columns = pl.ds(pl.multiple_of(q * feat, feat), feat)
            return dot(bg[...], w2[:, columns]).astype(BF16)

        pout[k] = part(chunk(k, False))
        pair(k).start()
        pown[k] = part(chunk(k, True))

    def calc_pair(k):
        def one(i, _):
            calc(k + i * (nz - 2 * k))
            return 0

        lax.fori_loop(0, 2, one, 0)

    def put(k, h, arrived):
        rows = pl.ds(h * half_rows, half_rows)
        value = pown[k, rows, :].astype(F32) + pin[k, rows, :].astype(F32)
        if arrived is not None:
            value = value + arrived[rows, :].astype(F32)
        sbuf[k, rows, :] = value.astype(BF16)

    def sum_right(k, h):
        return rcopy(
            half(sbuf.at[k], h), half(arr_r.at[k - 1], h), rs_rs.at[k - 1, h], rs_rr.at[k - 1, h], "tp", right
        )

    def sum_left(k, h):
        return rcopy(
            half(sbuf.at[nz - k], h), half(arr_l.at[k - 1], h), rs_ls.at[k - 1, h], rs_lr.at[k - 1, h], "tp", left
        )

    def tell(i, _):
        rcopy(cb.at[tp], cb.at[tp], cb_s, cb_r, "tp", lax.rem(tp + i, n_tp)).start()
        return 0

    calc(last)
    calc_pair(last - 1)
    cb[tp, :, :slots] = dot(jnp.ones((8, 128), F32), acch[...], NT, lax.Precision.HIGHEST)
    lax.fori_loop(1, n_tp, tell, 0)
    pair(last).wait_recv()
    put(last, 0, None)
    sum_right(last, 0).start()
    put(last, 1, None)
    sum_left(last, 1).start()
    for k in range(last - 1, 0, -1):
        first = k == last - 1
        pair(k).wait_recv()
        if not first:
            sum_right(k + 1, 1).wait_recv()
        put(k, 1, None if first else arr_r.at[k])
        sum_right(k, 1).start()
        pair(nz - k).wait_recv()
        if not first:
            sum_left(k + 1, 0).wait_recv()
        put(nz - k, 0, None if first else arr_l.at[k])
        sum_left(k, 0).start()
        if k > 1:
            calc_pair(k - 1)
        else:
            calc(0)
        sum_right(k + 1, 0).wait_recv()
        put(k, 0, arr_r.at[k])
        sum_right(k, 0).start()
        sum_left(k + 1, 1).wait_recv()
        put(nz - k, 1, arr_l.at[k])
        sum_left(k, 1).start()

    def down(q, _):
        columns = pl.ds(pl.multiple_of(q * feat, feat), feat)
        gd[:, columns] = dot(wt[...], fdy[q])[:hid].astype(BF16)
        return 0

    some = pl.ds(0, n_tp - 1)
    comb_all = rcopy(cb.at[some], cb.at[some], cb_s, cb_r, "tp", right)
    comb_all.wait_recv()
    comb_sum = jnp.sum(cb[...], axis=0)[:1, :slots]
    values = (places[2].astype(F32) * comb_sum).astype(BF16)
    _, slot_here = slot_of(iota((slots, 128), 0))
    extra = dot(values, ones_where(slot_here == iota((slots, 128), 1)))
    wt[...] = wcol[...].T.astype(BF16)
    pair(0).wait_recv()
    for h in (1, 0):
        sum_right(1, h).wait_recv()
        sum_left(1, h).wait_recv()
    total = pown[0].astype(F32) + pin[0].astype(F32) + arr_r[0].astype(F32) + arr_l[0].astype(F32)
    total = total.astype(BF16)
    for h in range(2):
        laid = dot(places[h], total[:, 128 * h : 128 * h + 128])
        if h == 0:
            laid = laid + extra
        s1[2, h] = laid.astype(BF16).reshape(side, side * ROWS, 128)
        swap(2, h, 0)
    lax.fori_loop(0, n_tp // 2, down, 0)
    for h in range(2):
        forward(2, h)
    lax.fori_loop(n_tp // 2, n_tp, down, 0)
    out = pltpu.make_async_copy(gd, gdown, gd_sem)
    out.start()

    for h in range(2):
        swapped(2, h, 1).wait_recv()
        back = r2[2, h].reshape(lines, 128)
        dtok[:, 128 * h : 128 * h + 128] = dot(hot[1 - h], back, TN).astype(BF16)
        if h == 0:
            column = iota((n_ep, lines), 1)
            told = dot(ones_where(iota((n_ep, lines), 0) * ROWS + CAP == column), back)
    by_expert = jnp.zeros((n_ep, tokens), F32)
    for k in range(CAP):
        by_expert = jnp.where(code[...] == k, told[:, k : k + 1], by_expert)
    for k in range(ids.shape[0]):
        hit = ids[k : k + 1, :] == expert
        dcomb[k : k + 1, :] = jnp.sum(jnp.where(hit, by_expert, 0.0), axis=0, keepdims=True)

    for t in range(5):
        for h in range(2):
            for phase in range(2):
                swapped(t, h, phase).wait_send()
    for t in range(2):
        to_opposite(t).wait_send()
        for j in range(last - 1):
            for h in range(2):
                to_right(t, j, h, mine).wait_send()
                to_left(t, j, h, mine).wait_send()
        for i in range(nz):
            to_sib(t, i, mine).wait_send()
    comb_all.wait_send()
    for k in range(nz):
        pair(k).wait_send()
    for k in range(1, last + 1):
        for h in range(2):
            if k < last or h == 0:
                sum_right(k, h).wait_send()
            if k < last or h == 1:
                sum_left(k, h).wait_send()
    out.wait()


def hand_over(tokens, combine, down, tokens_out, combine_out, down_out, a, b, c, in_sems, out_sems):
    part = down.shape[0] // 3
    moves = [(tokens, a, tokens_out), (combine, b, combine_out)]
    for i in range(3):
        rows = pl.ds(i * part, part)
        moves.append((down.at[rows], c.at[rows], down_out.at[rows]))
    inward = [pltpu.make_async_copy(x, y, in_sems.at[i]) for i, (x, y, _) in enumerate(moves)]
    outward = [pltpu.make_async_copy(y, z, out_sems.at[i]) for i, (_, y, z) in enumerate(moves)]
    for copy in inward:
        copy.start()
    for first, second in zip(inward, outward):
        first.wait()
        second.start()
    for copy in outward:
        copy.wait()


def per_device(n_ep, n_tp, tokens, grad_out, combine, expert_ids, w_gate, w_up, w_down):
    tok_count, feat = tokens.shape
    top = expert_ids.shape[1]
    hid, width = w_down.shape[1:]
    slots = n_ep * CAP
    nz = n_tp // 2
    side = math.isqrt(n_ep)
    vmem = pl.BlockSpec(memory_space=pltpu.VMEM)
    anyw = pl.BlockSpec(memory_space=pl.ANY)
    dma = pltpu.SemaphoreType.DMA
    blocks = pltpu.VMEM((5, 2, side, side * ROWS, 128), BF16)
    chunks = pltpu.VMEM((n_tp, slots, feat), BF16)
    parts = pltpu.VMEM((nz, slots, feat), BF16)
    results = pl.pallas_call(
        functools.partial(kernel, n_ep, n_tp),
        out_shape=(
            jax.ShapeDtypeStruct((tok_count, feat), BF16),
            jax.ShapeDtypeStruct((top, tok_count), F32),
            jax.ShapeDtypeStruct((hid, width), BF16),
        ),
        in_specs=[vmem] * 2 + [anyw] * 5,
        out_specs=(vmem, vmem, anyw),
        scratch_shapes=[
            pltpu.VMEM((tok_count, feat), BF16),
            pltpu.VMEM((tok_count, feat), BF16),
            pltpu.VMEM((2, tok_count, feat), BF16),
            pltpu.VMEM((256, width), BF16),
            pltpu.VMEM((128, width), BF16),
            pltpu.VMEM((2, n_ep * ROWS, tok_count), BF16),
            pltpu.VMEM((n_ep, tok_count), F32),
            pltpu.VMEM((3, slots, n_ep * ROWS), BF16),
            pltpu.VMEM((3, n_ep * ROWS, slots), BF16),
            blocks,
            blocks,
            blocks,
            blocks,
            chunks,
            chunks,
            pltpu.VMEM((slots, 256), F32),
            pltpu.VMEM((slots, 128), F32),
            pltpu.VMEM((slots, 128), F32),
            pltpu.VMEM((slots, 256), BF16),
            pltpu.VMEM((128, slots), BF16),
            pltpu.VMEM((n_tp, 8, 384), F32),
            parts,
            parts,
            parts,
            parts,
            pltpu.VMEM((nz // 2, slots, feat), BF16),
            pltpu.VMEM((nz // 2, slots, feat), BF16),
            pltpu.VMEM((hid, width), BF16),
            dma((5,)),
            dma((5, 2, 2)),
            dma((5, 2, 2)),
            dma((2, nz // 2 - 1, 2)),
            dma((2, nz // 2 - 1, 2)),
            dma((2, nz // 2 - 1, 2)),
            dma((2, nz // 2 - 1, 2)),
            dma((2, nz)),
            dma((2, nz)),
            dma((nz,)),
            dma((nz,)),
            dma((nz // 2, 2)),
            dma((nz // 2, 2)),
            dma((nz // 2, 2)),
            dma((nz // 2, 2)),
            dma,
            dma,
            dma,
            dma((2,)),
            dma((2,)),
        ],
        compiler_params=pltpu.CompilerParams(
            collective_id=0, has_side_effects=True, vmem_limit_bytes=60 * 1024 * 1024
        ),
    )(expert_ids.T, combine.T, tokens, grad_out, w_gate[0].T, w_up[0].T, w_down[0])
    d_tokens, d_combine, down = pl.pallas_call(
        hand_over,
        out_shape=tuple(jax.ShapeDtypeStruct(r.shape, r.dtype) for r in results),
        in_specs=[anyw] * 3,
        out_specs=(anyw,) * 3,
        scratch_shapes=[pltpu.VMEM(r.shape, r.dtype) for r in results] + [dma((5,)), dma((5,))],
        compiler_params=pltpu.CompilerParams(vmem_limit_bytes=60 * 1024 * 1024),
    )(*results)
    return d_tokens, d_combine.T, down[None]


def solution(mesh):
    placed = (
        P("ep", "tp"),
        P("ep", "tp"),
        P("ep", None),
        P("ep", None),
        P("ep", None, "tp"),
        P("ep", None, "tp"),
        P("ep", "tp", None),
    )
    return jax.shard_map(
        functools.partial(per_device, mesh.shape["ep"], mesh.shape["tp"]),
        mesh=mesh,
        in_specs=placed,
        out_specs=(P("ep", "tp"), P("ep", None), P("ep", "tp", None)),
        check_vma=False,
    )
```

```python
import functools
import math

import jax
import jax.numpy as jnp
from jax import lax
from jax.experimental import pallas as pl
from jax.experimental.pallas import tpu as pltpu
from jax.sharding import PartitionSpec as P

MESH = pl.DeviceIdType.MESH
F32 = jnp.float32
BF16 = jnp.bfloat16
CAP = 5
ROWS = 6
NN = (((1,), (0,)), ((), ()))
NT = (((1,), (1,)), ((), ()))
TN = (((0,), (0,)), ((), ()))


def dot(a, b, dims=NN, precision=None):
    return lax.dot_general(a, b, dims, preferred_element_type=F32, precision=precision)


def iota(shape, dim):
    return lax.broadcasted_iota(jnp.int32, shape, dim)


def where_block(u, swapped, side):
    return (u & (side - 1)) * side + lax.div(u, side) if swapped else u


def slot_of(i):
    s = (i * 3277) >> 14
    return s, i - s * CAP


def block_of(r):
    u = (r * 10923) >> 16
    return u, r - u * ROWS


def ones_where(mask):
    return jnp.where(mask, 1.0, 0.0).astype(BF16)


def kernel(
    n_ep,
    n_tp,
    ids,
    comb,
    tok_hbm,
    gout_hbm,
    wg,
    wu,
    wd,
    dtok,
    dcomb,
    gdown,
    tok,
    gout,
    far,
    w2,
    wdp,
    hot,
    code,
    picks,
    places,
    s1,
    r1,
    s2,
    r2,
    fx,
    fdy,
    acc,
    acch,
    wcol,
    bg,
    wt,
    cb,
    pown,
    pout,
    pin,
    sbuf,
    arr_r,
    arr_l,
    gd,
    w_sem,
    ep_s,
    ep_r,
    ag_rs,
    ag_rr,
    ag_ls,
    ag_lr,
    sib_s,
    sib_r,
    pair_s,
    pair_r,
    rs_rs,
    rs_rr,
    rs_ls,
    rs_lr,
    cb_s,
    cb_r,
    gd_sem,
    far_s,
    far_r,
    far_out,
    far_in,
):
    side = s1.shape[2]
    nz = n_tp // 2
    ep = lax.axis_index("ep")
    tp = lax.axis_index("tp")
    gx = lax.div(ep, side)
    gy = lax.rem(ep, side)
    z = lax.div(tp, 2)
    c = lax.rem(tp, 2)
    right = lax.rem(z + 1, nz) * 2 + c
    left = lax.rem(z + nz - 1, nz) * 2 + c
    sib = z * 2 + 1 - c
    opposite = lax.rem(z + nz // 2, nz) * 2 + c
    slots = fx.shape[1]
    feat = fx.shape[2]
    half_rows = slots // 2
    hid = wg.shape[0]
    lines = n_ep * ROWS

    def rcopy(src, dst, s, r, axis, to):
        return pltpu.make_async_remote_copy(
            src_ref=src, dst_ref=dst, send_sem=s, recv_sem=r, device_id={axis: to}, device_id_type=MESH
        )

    def neighbour(i, along_y):
        if along_y:
            return gx * side + lax.rem(gy + i, side)
        return lax.rem(gx + i, side) * side + gy

    loads = (
        pltpu.make_async_copy(tok_hbm, tok, w_sem.at[0]),
        pltpu.make_async_copy(gout_hbm, gout, w_sem.at[1]),
        pltpu.make_async_copy(wg, w2.at[pl.ds(0, hid)], w_sem.at[2]),
        pltpu.make_async_copy(wu, w2.at[pl.ds(128, hid)], w_sem.at[3]),
        pltpu.make_async_copy(wd, wdp.at[pl.ds(0, hid)], w_sem.at[4]),
    )
    for load in loads:
        load.start()

    barrier = pltpu.get_barrier_semaphore()

    def greet_y(i, _):
        pl.semaphore_signal(barrier, inc=1, device_id={"ep": neighbour(i, True)}, device_id_type=MESH)
        return 0

    def greet_x(i, _):
        pl.semaphore_signal(barrier, inc=1, device_id={"ep": neighbour(i, False)}, device_id_type=MESH)
        return 0

    def greet_tp(i, _):
        pl.semaphore_signal(barrier, inc=1, device_id={"tp": lax.rem(tp + i, n_tp)}, device_id_type=MESH)
        return 0

    lax.fori_loop(1, side, greet_y, 0)
    lax.fori_loop(1, side, greet_x, 0)
    lax.fori_loop(1, n_tp, greet_tp, 0)

    tokens = tok.shape[0]
    expert = iota((n_ep, tokens), 0)
    named = jnp.zeros((n_ep, tokens), F32)
    weight = jnp.zeros((n_ep, tokens), F32)
    for k in range(ids.shape[0]):
        hit = ids[k : k + 1, :] == expert
        named = jnp.where(hit, 1.0, named)
        weight = jnp.where(hit, comb[k : k + 1, :].astype(F32), weight)
    earlier = ones_where(iota((tokens, tokens), 0) < iota((tokens, tokens), 1))
    rank = dot(named.astype(BF16), earlier)
    code[...] = jnp.where(named > 0.5, rank, 99.0)
    lane = iota((n_ep, 128), 1)
    scalars = jnp.zeros((n_ep, 128), F32)
    for k in range(CAP):
        one = jnp.sum(jnp.where(code[...] == k, weight, 0.0), axis=1, keepdims=True)
        scalars = jnp.where(lane == k, one, scalars)
    block, line = block_of(iota((lines, n_ep), 0))
    _, line_t = block_of(iota((lines, tokens), 0))
    for h in range(2):
        spread = where_block(block, h == 0, side) == iota((lines, n_ep), 1)
        rows = dot(ones_where(spread), code[...].astype(BF16))
        hot[h] = ones_where(rows == line_t.astype(F32))
        if h == 0:
            extra = dot(ones_where(spread & (line == CAP)), scalars.astype(BF16))

    def lay(t, tokens_of, more):
        for h in range(2):
            laid = dot(hot[h], tokens_of[:, 128 * h : 128 * h + 128])
            if h == 0 and more is not None:
                laid = laid + more
            s1[t, h] = laid.astype(BF16).reshape(side, side * ROWS, 128)

    loads[0].wait()
    lay(0, tok, extra)

    pl.semaphore_wait(barrier, 2 * (side - 1) + n_tp - 1)

    out_of, into = (s1, s2), (r1, r2)

    def swap(t, h, phase):
        along_y = (h == 0) == (phase == 0)
        me = gy if along_y else gx
        src, dst = out_of[phase], into[phase]

        def one(i, _):
            to = lax.rem(me + i, side)
            rcopy(
                src.at[t, h, to],
                dst.at[t, h, me],
                ep_s.at[t, h, phase],
                ep_r.at[t, h, phase],
                "ep",
                neighbour(i, along_y),
            ).start()
            return 0

        lax.fori_loop(1, side, one, 0)
        dst[t, h, pl.ds(me, 1)] = src[t, h, pl.ds(me, 1)]

    def swapped(t, h, phase):
        some = pl.ds(0, side - 1)
        return rcopy(
            out_of[phase].at[t, h, some],
            into[phase].at[t, h, some],
            ep_s.at[t, h, phase],
            ep_r.at[t, h, phase],
            "ep",
            neighbour(1, (h == 0) == (phase == 0)),
        )

    def to_opposite(t):
        return rcopy((tok, gout)[t], far.at[t], far_s.at[t], far_r.at[t], "tp", opposite)

    swap(0, 0, 0)
    swap(0, 1, 0)
    loads[1].wait()
    lay(1, gout, None)
    swap(1, 0, 0)
    swap(1, 1, 0)
    to_opposite(0).start()
    to_opposite(1).start()

    gap = 128 - hid
    blank = jnp.zeros((gap, w2.shape[1]), BF16)
    w2[pl.ds(hid, gap), :] = blank
    w2[pl.ds(128 + hid, gap), :] = blank
    wdp[pl.ds(hid, gap), :] = blank
    acc[...] = jnp.zeros_like(acc)
    acch[...] = jnp.zeros_like(acch)
    block, line = block_of(iota((lines, lines), 0))
    turn = ones_where(where_block(block, True, side) * ROWS + line == iota((lines, lines), 1))

    source, slot = slot_of(iota((slots, lines), 0))
    column = iota((slots, lines), 1)
    picks[0] = ones_where(source * ROWS + slot == column)
    picks[1] = ones_where(where_block(source, True, side) * ROWS + slot == column)
    picks[2] = ones_where(source * ROWS + CAP == column)

    def forward(t, h):
        swapped(t, h, 0).wait_recv()
        turned = dot(turn, r1[t, h].reshape(lines, 128))
        s2[t, h] = turned.astype(BF16).reshape(side, side * ROWS, 128)
        swap(t, h, 1)

    for t in range(2):
        for h in range(2):
            forward(t, h)
    for load in loads[2:]:
        load.wait()

    full = (fx, fdy)
    last = nz // 2

    def half(ref, h):
        return ref.at[pl.ds(h * half_rows, half_rows)]

    def chunk(k, own):
        return lax.rem(z + k + nz, nz) * 2 + (c if own else 1 - c)

    def to_right(t, j, h, q):
        piece = half(full[t].at[q], h)
        return rcopy(piece, piece, ag_rs.at[t, j, h], ag_rr.at[t, j, h], "tp", right)

    def to_left(t, j, h, q):
        piece = half(full[t].at[q], h)
        return rcopy(piece, piece, ag_ls.at[t, j, h], ag_lr.at[t, j, h], "tp", left)

    def to_sib(t, i, q):
        piece = full[t].at[q]
        return rcopy(piece, piece, sib_s.at[t, i], sib_r.at[t, i], "tp", sib)

    def consume(t, q):
        columns = pl.ds(pl.multiple_of(q * feat, feat), feat)
        if t == 0:
            acc[...] += dot(fx[q], w2[:, columns], NT)
        else:
            acch[...] += dot(fdy[q], wdp[:, columns], NT)

    def consume_pair(t, j, own):
        def one(i, _):
            consume(t, chunk(j * (2 * i - 1), own))
            return 0

        lax.fori_loop(0, 2, one, 0)

    mine = chunk(0, True)

    def unpack(t, blocks, q):
        for h in range(2):
            swapped(blocks, h, 1).wait_recv()
            packed = dot(picks[h], r2[blocks, h].reshape(lines, 128))
            full[t][q, :, 128 * h : 128 * h + 128] = packed.astype(BF16)

    def own_chunk(t):
        unpack(t, t, mine)
        to_right(t, 0, 0, mine).start()
        to_left(t, 0, 1, mine).start()
        to_right(t, 0, 1, mine).start()
        to_left(t, 0, 0, mine).start()
        to_sib(t, 0, mine).start()
        consume(t, mine)

    def arrival(t, j):
        from_left, from_right = chunk(-j, True), chunk(j, True)
        for h in range(2):
            to_right(t, j - 1, h, from_left).wait_recv()
            if j < last - 1:
                to_right(t, j, h, from_left).start()
            to_left(t, j - 1, 1 - h, from_right).wait_recv()
            if j < last - 1:
                to_left(t, j, 1 - h, from_right).start()
        to_sib(t, j, from_left).start()
        to_sib(t, last + j, from_right).start()
        consume_pair(t, j, True)

    def from_sib(t, j):
        to_sib(t, j, chunk(-j, False)).wait_recv()
        if 0 < j < last:
            to_sib(t, last + j, chunk(j, False)).wait_recv()
            consume_pair(t, j, False)
        else:
            consume(t, chunk(j, False))

    def farthest(t):
        q = chunk(last, True)
        unpack(t, 3 + t, q)
        to_sib(t, last, q).start()
        consume(t, q)

    own_chunk(0)
    own_chunk(1)
    picked = dot(picks[2], r2[0, 0].reshape(lines, 128))
    _, slot_here = slot_of(iota((slots, 128), 0))
    picked = jnp.where(iota((slots, 128), 1) == slot_here, picked, 0.0).astype(BF16)
    wcol[...] = dot(picked, jnp.ones((128, 128), BF16))
    for t in range(2):
        to_opposite(t).wait_recv()
        lay(3 + t, far.at[t], None)
        swap(3 + t, 0, 0)
        swap(3 + t, 1, 0)
    for t in range(2):
        arrival(t, 1)
    for t in range(2):
        for h in range(2):
            forward(3 + t, h)
    for t in range(2):
        from_sib(t, 0)
        from_sib(t, 1)
    for t in range(2):
        arrival(t, 2)
    source, slot = slot_of(iota((lines, slots), 1))
    row = iota((lines, slots), 0)
    major = where_block(source, True, side) * ROWS
    places[0] = ones_where(row == major + slot)
    places[1] = ones_where(row == source * ROWS + slot)
    places[2] = ones_where(row == major + CAP)
    for t in range(2):
        farthest(t)
        from_sib(t, 2)
    for t in range(2):
        arrival(t, 3)
    for t in range(2):
        from_sib(t, last)
        from_sib(t, 3)

    for g in range(slots // 80):
        rows = pl.ds(80 * g, 80)
        gate, up, back = acc[rows, :128], acc[rows, 128:], acch[rows, :]
        w = wcol[rows, :]
        sigma = jax.nn.sigmoid(gate)
        act = gate * sigma
        product = act * up
        scaled = w * back
        bg[rows, :128] = (scaled * up * sigma * (1.0 + gate * (1.0 - sigma))).astype(BF16)
        bg[rows, 128:] = (scaled * act).astype(BF16)
        acch[rows, :] = product.astype(BF16).astype(F32) * back
        wcol[rows, :] = w * product

    def pair(k):
        return rcopy(pout.at[k], pin.at[k], pair_s.at[k], pair_r.at[k], "tp", sib)

    def calc(k):
        def part(q):
            columns = pl.ds(pl.multiple_of(q * feat, feat), feat)
            return dot(bg[...], w2[:, columns]).astype(BF16)

        pout[k] = part(chunk(k, False))
        pair(k).start()
        pown[k] = part(chunk(k, True))

    def calc_pair(k):
        def one(i, _):
            calc(k + i * (nz - 2 * k))
            return 0

        lax.fori_loop(0, 2, one, 0)

    def put(k, h, arrived):
        rows = pl.ds(h * half_rows, half_rows)
        value = pown[k, rows, :].astype(F32) + pin[k, rows, :].astype(F32)
        if arrived is not None:
            value = value + arrived[rows, :].astype(F32)
        sbuf[k, rows, :] = value.astype(BF16)

    def sum_right(k, h):
        return rcopy(
            half(sbuf.at[k], h), half(arr_r.at[k - 1], h), rs_rs.at[k - 1, h], rs_rr.at[k - 1, h], "tp", right
        )

    def sum_left(k, h):
        return rcopy(
            half(sbuf.at[nz - k], h), half(arr_l.at[k - 1], h), rs_ls.at[k - 1, h], rs_lr.at[k - 1, h], "tp", left
        )

    def tell(i, _):
        rcopy(cb.at[tp], cb.at[tp], cb_s, cb_r, "tp", lax.rem(tp + i, n_tp)).start()
        return 0

    def lay_sums(t, total, more):
        for h in range(2):
            laid = dot(places[h], total[:, 128 * h : 128 * h + 128])
            if h == 0 and more is not None:
                laid = laid + more
            s1[t, h] = laid.astype(BF16).reshape(side, side * ROWS, 128)
            swap(t, h, 0)

    calc_pair(last - 1)
    calc(last)
    for k in range(last - 1, 0, -1):
        first = k == last - 1
        for h in range(2):
            if first and h == 0:
                pair(k).wait_recv()
            elif not first:
                if h == 0:
                    pair(k).wait_recv()
                sum_right(k + 1, 1 - h).wait_recv()
            put(k, 1 - h, None if first else arr_r.at[k])
            sum_right(k, 1 - h).start()
            if h == 0:
                pair(nz - k).wait_recv()
            if not first:
                sum_left(k + 1, h).wait_recv()
            put(nz - k, h, None if first else arr_l.at[k])
            sum_left(k, h).start()
            if h == 0 and not first:
                if k > 1:
                    calc_pair(k - 1)
                else:
                    calc(0)
        if first:
            cb[tp, :, :slots] = dot(jnp.ones((8, 128), F32), acch[...], NT, lax.Precision.HIGHEST)
            lax.fori_loop(1, n_tp, tell, 0)
            calc_pair(k - 1)
            pair(last).wait_recv()
            lay_sums(5, (pown[last].astype(F32) + pin[last].astype(F32)).astype(BF16), None)
        elif k == 2:
            for h in range(2):
                forward(5, h)

    def down(q, _):
        columns = pl.ds(pl.multiple_of(q * feat, feat), feat)
        gd[:, columns] = dot(wt[...], fdy[q])[:hid].astype(BF16)
        return 0

    some = pl.ds(0, n_tp - 1)
    comb_all = rcopy(cb.at[some], cb.at[some], cb_s, cb_r, "tp", right)
    comb_all.wait_recv()
    comb_sum = jnp.sum(cb[...], axis=0)[:1, :slots]
    values = (places[2].astype(F32) * comb_sum).astype(BF16)
    _, slot_here = slot_of(iota((slots, 128), 0))
    extra = dot(values, ones_where(slot_here == iota((slots, 128), 1)))
    wt[...] = wcol[...].T.astype(BF16)
    pair(0).wait_recv()
    for h in (1, 0):
        sum_right(1, h).wait_recv()
        sum_left(1, h).wait_recv()
    total = pown[0].astype(F32) + pin[0].astype(F32) + arr_r[0].astype(F32) + arr_l[0].astype(F32)
    lay_sums(2, total.astype(BF16), extra)
    for h in range(2):
        swapped(5, h, 1).wait_recv()
        far_out[:, 128 * h : 128 * h + 128] = dot(hot[1 - h], r2[5, h].reshape(lines, 128), TN)
    cross = rcopy(far_out, far_in, far_s.at[2], far_r.at[2], "tp", opposite)
    cross.start()
    lax.fori_loop(0, n_tp // 2, down, 0)
    for h in range(2):
        forward(2, h)
    lax.fori_loop(n_tp // 2, n_tp, down, 0)
    out = pltpu.make_async_copy(gd, gdown, gd_sem)
    out.start()

    cross.wait_recv()
    for h in range(2):
        swapped(2, h, 1).wait_recv()
        back = r2[2, h].reshape(lines, 128)
        summed = dot(hot[1 - h], back, TN) + far_in[:, 128 * h : 128 * h + 128]
        dtok[:, 128 * h : 128 * h + 128] = summed.astype(BF16)
        if h == 0:
            column = iota((n_ep, lines), 1)
            told = dot(ones_where(iota((n_ep, lines), 0) * ROWS + CAP == column), back)
    by_expert = jnp.zeros((n_ep, tokens), F32)
    for k in range(CAP):
        by_expert = jnp.where(code[...] == k, told[:, k : k + 1], by_expert)
    for k in range(ids.shape[0]):
        hit = ids[k : k + 1, :] == expert
        dcomb[k : k + 1, :] = jnp.sum(jnp.where(hit, by_expert, 0.0), axis=0, keepdims=True)

    for t in range(6):
        for h in range(2):
            for phase in range(2):
                swapped(t, h, phase).wait_send()
    for t in range(2):
        to_opposite(t).wait_send()
        for j in range(last - 1):
            for h in range(2):
                to_right(t, j, h, mine).wait_send()
                to_left(t, j, h, mine).wait_send()
        for i in range(nz):
            to_sib(t, i, mine).wait_send()
    comb_all.wait_send()
    for k in range(nz):
        pair(k).wait_send()
    for k in range(1, last):
        for h in range(2):
            sum_right(k, h).wait_send()
            sum_left(k, h).wait_send()
    cross.wait_send()
    out.wait()


def hand_over(tokens, combine, down, tokens_out, combine_out, down_out, a, b, c, in_sems, out_sems):
    part = down.shape[0] // 3
    moves = [(tokens, a, tokens_out), (combine, b, combine_out)]
    for i in range(3):
        rows = pl.ds(i * part, part)
        moves.append((down.at[rows], c.at[rows], down_out.at[rows]))
    inward = [pltpu.make_async_copy(x, y, in_sems.at[i]) for i, (x, y, _) in enumerate(moves)]
    outward = [pltpu.make_async_copy(y, z, out_sems.at[i]) for i, (_, y, z) in enumerate(moves)]
    for copy in inward:
        copy.start()
    for first, second in zip(inward, outward):
        first.wait()
        second.start()
    for copy in outward:
        copy.wait()


def per_device(n_ep, n_tp, tokens, grad_out, combine, expert_ids, w_gate, w_up, w_down):
    tok_count, feat = tokens.shape
    top = expert_ids.shape[1]
    hid, width = w_down.shape[1:]
    slots = n_ep * CAP
    nz = n_tp // 2
    side = math.isqrt(n_ep)
    vmem = pl.BlockSpec(memory_space=pltpu.VMEM)
    anyw = pl.BlockSpec(memory_space=pl.ANY)
    dma = pltpu.SemaphoreType.DMA
    blocks = pltpu.VMEM((6, 2, side, side * ROWS, 128), BF16)
    chunks = pltpu.VMEM((n_tp, slots, feat), BF16)
    parts = pltpu.VMEM((nz, slots, feat), BF16)
    results = pl.pallas_call(
        functools.partial(kernel, n_ep, n_tp),
        out_shape=(
            jax.ShapeDtypeStruct((tok_count, feat), BF16),
            jax.ShapeDtypeStruct((top, tok_count), F32),
            jax.ShapeDtypeStruct((hid, width), BF16),
        ),
        in_specs=[vmem] * 2 + [anyw] * 5,
        out_specs=(vmem, vmem, anyw),
        scratch_shapes=[
            pltpu.VMEM((tok_count, feat), BF16),
            pltpu.VMEM((tok_count, feat), BF16),
            pltpu.VMEM((2, tok_count, feat), BF16),
            pltpu.VMEM((256, width), BF16),
            pltpu.VMEM((128, width), BF16),
            pltpu.VMEM((2, n_ep * ROWS, tok_count), BF16),
            pltpu.VMEM((n_ep, tok_count), F32),
            pltpu.VMEM((3, slots, n_ep * ROWS), BF16),
            pltpu.VMEM((3, n_ep * ROWS, slots), BF16),
            blocks,
            blocks,
            blocks,
            blocks,
            chunks,
            chunks,
            pltpu.VMEM((slots, 256), F32),
            pltpu.VMEM((slots, 128), F32),
            pltpu.VMEM((slots, 128), F32),
            pltpu.VMEM((slots, 256), BF16),
            pltpu.VMEM((128, slots), BF16),
            pltpu.VMEM((n_tp, 8, 384), F32),
            parts,
            parts,
            parts,
            parts,
            pltpu.VMEM((nz // 2, slots, feat), BF16),
            pltpu.VMEM((nz // 2, slots, feat), BF16),
            pltpu.VMEM((hid, width), BF16),
            dma((5,)),
            dma((6, 2, 2)),
            dma((6, 2, 2)),
            dma((2, nz // 2 - 1, 2)),
            dma((2, nz // 2 - 1, 2)),
            dma((2, nz // 2 - 1, 2)),
            dma((2, nz // 2 - 1, 2)),
            dma((2, nz)),
            dma((2, nz)),
            dma((nz,)),
            dma((nz,)),
            dma((nz // 2, 2)),
            dma((nz // 2, 2)),
            dma((nz // 2, 2)),
            dma((nz // 2, 2)),
            dma,
            dma,
            dma,
            dma((3,)),
            dma((3,)),
            pltpu.VMEM((tok_count, feat), F32),
            pltpu.VMEM((tok_count, feat), F32),
        ],
        compiler_params=pltpu.CompilerParams(
            collective_id=0, has_side_effects=True, vmem_limit_bytes=60 * 1024 * 1024
        ),
    )(expert_ids.T, combine.T, tokens, grad_out, w_gate[0].T, w_up[0].T, w_down[0])
    d_tokens, d_combine, down = pl.pallas_call(
        hand_over,
        out_shape=tuple(jax.ShapeDtypeStruct(r.shape, r.dtype) for r in results),
        in_specs=[anyw] * 3,
        out_specs=(anyw,) * 3,
        scratch_shapes=[pltpu.VMEM(r.shape, r.dtype) for r in results] + [dma((5,)), dma((5,))],
        compiler_params=pltpu.CompilerParams(vmem_limit_bytes=60 * 1024 * 1024),
    )(*results)
    return d_tokens, d_combine.T, down[None]


def solution(mesh):
    placed = (
        P("ep", "tp"),
        P("ep", "tp"),
        P("ep", None),
        P("ep", None),
        P("ep", None, "tp"),
        P("ep", None, "tp"),
        P("ep", "tp", None),
    )
    return jax.shard_map(
        functools.partial(per_device, mesh.shape["ep"], mesh.shape["tp"]),
        mesh=mesh,
        in_specs=placed,
        out_specs=(P("ep", "tp"), P("ep", None), P("ep", "tp", None)),
        check_vma=False,
    )
```

```python
import functools
import math

import jax
import jax.numpy as jnp
from jax import lax
from jax.experimental import pallas as pl
from jax.experimental.pallas import tpu as pltpu
from jax.sharding import PartitionSpec as P

MESH = pl.DeviceIdType.MESH
F32 = jnp.float32
BF16 = jnp.bfloat16
CAP = 5
ROWS = 6
NN = (((1,), (0,)), ((), ()))
NT = (((1,), (1,)), ((), ()))
TN = (((0,), (0,)), ((), ()))


def dot(a, b, dims=NN, precision=None):
    return lax.dot_general(a, b, dims, preferred_element_type=F32, precision=precision)


def iota(shape, dim):
    return lax.broadcasted_iota(jnp.int32, shape, dim)


def where_block(u, swapped, side):
    return (u & (side - 1)) * side + lax.div(u, side) if swapped else u


def slot_of(i):
    s = (i * 3277) >> 14
    return s, i - s * CAP


def block_of(r):
    u = (r * 10923) >> 16
    return u, r - u * ROWS


def ones_where(mask):
    return jnp.where(mask, 1.0, 0.0).astype(BF16)


def kernel(
    n_ep,
    n_tp,
    ids,
    comb,
    tok_hbm,
    gout_hbm,
    wg,
    wu,
    wd,
    dtok,
    dcomb,
    gdown,
    tok,
    gout,
    far,
    w2,
    wdp,
    hot,
    code,
    picks,
    places,
    s1,
    r1,
    s2,
    r2,
    fx,
    fdy,
    acc,
    acch,
    wcol,
    bg,
    wt,
    cb,
    pown,
    pout,
    pin,
    sbuf,
    arr_r,
    arr_l,
    gd,
    w_sem,
    ep_s,
    ep_r,
    ag_rs,
    ag_rr,
    ag_ls,
    ag_lr,
    sib_s,
    sib_r,
    pair_s,
    pair_r,
    rs_rs,
    rs_rr,
    rs_ls,
    rs_lr,
    cb_s,
    cb_r,
    gd_sem,
    far_s,
    far_r,
    far_out,
    far_in,
):
    side = s1.shape[2]
    nz = n_tp // 2
    ep = lax.axis_index("ep")
    tp = lax.axis_index("tp")
    gx = lax.div(ep, side)
    gy = lax.rem(ep, side)
    z = lax.div(tp, 2)
    c = lax.rem(tp, 2)
    right = lax.rem(z + 1, nz) * 2 + c
    left = lax.rem(z + nz - 1, nz) * 2 + c
    sib = z * 2 + 1 - c
    opposite = lax.rem(z + nz // 2, nz) * 2 + c
    slots = fx.shape[1]
    feat = fx.shape[2]
    half_rows = slots // 2
    hid = wg.shape[0]
    lines = n_ep * ROWS

    def rcopy(src, dst, s, r, axis, to):
        return pltpu.make_async_remote_copy(
            src_ref=src, dst_ref=dst, send_sem=s, recv_sem=r, device_id={axis: to}, device_id_type=MESH
        )

    def neighbour(i, along_y):
        if along_y:
            return gx * side + lax.rem(gy + i, side)
        return lax.rem(gx + i, side) * side + gy

    loads = (
        pltpu.make_async_copy(tok_hbm, tok, w_sem.at[0]),
        pltpu.make_async_copy(gout_hbm, gout, w_sem.at[1]),
        pltpu.make_async_copy(wg, w2.at[pl.ds(0, hid)], w_sem.at[2]),
        pltpu.make_async_copy(wu, w2.at[pl.ds(128, hid)], w_sem.at[3]),
        pltpu.make_async_copy(wd, wdp.at[pl.ds(0, hid)], w_sem.at[4]),
    )
    for load in loads:
        load.start()

    barrier = pltpu.get_barrier_semaphore()

    def greet_y(i, _):
        pl.semaphore_signal(barrier, inc=1, device_id={"ep": neighbour(i, True)}, device_id_type=MESH)
        return 0

    def greet_x(i, _):
        pl.semaphore_signal(barrier, inc=1, device_id={"ep": neighbour(i, False)}, device_id_type=MESH)
        return 0

    def greet_tp(i, _):
        pl.semaphore_signal(barrier, inc=1, device_id={"tp": lax.rem(tp + i, n_tp)}, device_id_type=MESH)
        return 0

    lax.fori_loop(1, side, greet_y, 0)
    lax.fori_loop(1, side, greet_x, 0)
    lax.fori_loop(1, n_tp, greet_tp, 0)

    tokens = tok.shape[0]
    expert = iota((n_ep, tokens), 0)
    named = jnp.zeros((n_ep, tokens), F32)
    weight = jnp.zeros((n_ep, tokens), F32)
    for k in range(ids.shape[0]):
        hit = ids[k : k + 1, :] == expert
        named = jnp.where(hit, 1.0, named)
        weight = jnp.where(hit, comb[k : k + 1, :].astype(F32), weight)
    earlier = ones_where(iota((tokens, tokens), 0) < iota((tokens, tokens), 1))
    rank = dot(named.astype(BF16), earlier)
    code[...] = jnp.where(named > 0.5, rank, 99.0)
    lane = iota((n_ep, 128), 1)
    scalars = jnp.zeros((n_ep, 128), F32)
    for k in range(CAP):
        one = jnp.sum(jnp.where(code[...] == k, weight, 0.0), axis=1, keepdims=True)
        scalars = jnp.where(lane == k, one, scalars)
    block, line = block_of(iota((lines, n_ep), 0))
    _, line_t = block_of(iota((lines, tokens), 0))
    for h in range(2):
        spread = where_block(block, h == 0, side) == iota((lines, n_ep), 1)
        rows = dot(ones_where(spread), code[...].astype(BF16))
        hot[h] = ones_where(rows == line_t.astype(F32))
        if h == 0:
            extra = dot(ones_where(spread & (line == CAP)), scalars.astype(BF16))

    def lay(t, tokens_of, more):
        for h in range(2):
            laid = dot(hot[h], tokens_of[:, 128 * h : 128 * h + 128])
            if h == 0 and more is not None:
                laid = laid + more
            s1[t, h] = laid.astype(BF16).reshape(side, side * ROWS, 128)

    loads[0].wait()
    lay(0, tok, extra)

    pl.semaphore_wait(barrier, 2 * (side - 1) + n_tp - 1)

    out_of, into = (s1, s2), (r1, r2)

    def swap(t, h, phase):
        along_y = (h == 0) == (phase == 0)
        me = gy if along_y else gx
        src, dst = out_of[phase], into[phase]

        def one(i, _):
            to = lax.rem(me + i, side)
            rcopy(
                src.at[t, h, to],
                dst.at[t, h, me],
                ep_s.at[t, h, phase],
                ep_r.at[t, h, phase],
                "ep",
                neighbour(i, along_y),
            ).start()
            return 0

        lax.fori_loop(1, side, one, 0)
        dst[t, h, pl.ds(me, 1)] = src[t, h, pl.ds(me, 1)]

    def swapped(t, h, phase):
        some = pl.ds(0, side - 1)
        return rcopy(
            out_of[phase].at[t, h, some],
            into[phase].at[t, h, some],
            ep_s.at[t, h, phase],
            ep_r.at[t, h, phase],
            "ep",
            neighbour(1, (h == 0) == (phase == 0)),
        )

    def to_opposite(t):
        return rcopy((tok, gout)[t], far.at[t], far_s.at[t], far_r.at[t], "tp", opposite)

    swap(0, 0, 0)
    swap(0, 1, 0)
    loads[1].wait()
    lay(1, gout, None)
    swap(1, 0, 0)
    swap(1, 1, 0)
    to_opposite(0).start()
    to_opposite(1).start()

    gap = 128 - hid
    blank = jnp.zeros((gap, w2.shape[1]), BF16)
    w2[pl.ds(hid, gap), :] = blank
    w2[pl.ds(128 + hid, gap), :] = blank
    wdp[pl.ds(hid, gap), :] = blank
    acc[...] = jnp.zeros_like(acc)
    acch[...] = jnp.zeros_like(acch)
    block, line = block_of(iota((lines, lines), 0))
    turn = ones_where(where_block(block, True, side) * ROWS + line == iota((lines, lines), 1))

    source, slot = slot_of(iota((slots, lines), 0))
    column = iota((slots, lines), 1)
    picks[0] = ones_where(source * ROWS + slot == column)
    picks[1] = ones_where(where_block(source, True, side) * ROWS + slot == column)
    picks[2] = ones_where(source * ROWS + CAP == column)

    def forward(t, h):
        swapped(t, h, 0).wait_recv()
        turned = dot(turn, r1[t, h].reshape(lines, 128))
        s2[t, h] = turned.astype(BF16).reshape(side, side * ROWS, 128)
        swap(t, h, 1)

    for t in range(2):
        for h in range(2):
            forward(t, h)
    for load in loads[2:]:
        load.wait()

    full = (fx, fdy)
    last = nz // 2

    def half(ref, h):
        return ref.at[pl.ds(h * half_rows, half_rows)]

    def chunk(k, own):
        return lax.rem(z + k + nz, nz) * 2 + (c if own else 1 - c)

    def to_right(t, j, h, q):
        piece = half(full[t].at[q], h)
        return rcopy(piece, piece, ag_rs.at[t, j, h], ag_rr.at[t, j, h], "tp", right)

    def to_left(t, j, h, q):
        piece = half(full[t].at[q], h)
        return rcopy(piece, piece, ag_ls.at[t, j, h], ag_lr.at[t, j, h], "tp", left)

    def to_sib(t, i, q):
        piece = full[t].at[q]
        return rcopy(piece, piece, sib_s.at[t, i], sib_r.at[t, i], "tp", sib)

    def consume(t, q):
        columns = pl.ds(pl.multiple_of(q * feat, feat), feat)
        if t == 0:
            acc[...] += dot(fx[q], w2[:, columns], NT)
        else:
            acch[...] += dot(fdy[q], wdp[:, columns], NT)

    def consume_pair(t, j, own):
        def one(i, _):
            consume(t, chunk(j * (2 * i - 1), own))
            return 0

        lax.fori_loop(0, 2, one, 0)

    mine = chunk(0, True)

    def unpack(t, blocks, q):
        for h in range(2):
            swapped(blocks, h, 1).wait_recv()
            packed = dot(picks[h], r2[blocks, h].reshape(lines, 128))
            full[t][q, :, 128 * h : 128 * h + 128] = packed.astype(BF16)

    def own_chunk(t):
        unpack(t, t, mine)
        to_right(t, 0, 0, mine).start()
        to_left(t, 0, 1, mine).start()
        to_right(t, 0, 1, mine).start()
        to_left(t, 0, 0, mine).start()
        to_sib(t, 0, mine).start()
        consume(t, mine)

    def arrival(t, j):
        from_left, from_right = chunk(-j, True), chunk(j, True)
        for h in range(2):
            to_right(t, j - 1, h, from_left).wait_recv()
            if j < last - 1:
                to_right(t, j, h, from_left).start()
            to_left(t, j - 1, 1 - h, from_right).wait_recv()
            if j < last - 1:
                to_left(t, j, 1 - h, from_right).start()
        to_sib(t, j, from_left).start()
        to_sib(t, last + j, from_right).start()
        consume_pair(t, j, True)

    def from_sib(t, j):
        to_sib(t, j, chunk(-j, False)).wait_recv()
        if 0 < j < last:
            to_sib(t, last + j, chunk(j, False)).wait_recv()
            consume_pair(t, j, False)
        else:
            consume(t, chunk(j, False))

    def farthest(t):
        q = chunk(last, True)
        unpack(t, 3 + t, q)
        to_sib(t, last, q).start()
        consume(t, q)

    own_chunk(0)
    own_chunk(1)
    picked = dot(picks[2], r2[0, 0].reshape(lines, 128))
    _, slot_here = slot_of(iota((slots, 128), 0))
    picked = jnp.where(iota((slots, 128), 1) == slot_here, picked, 0.0).astype(BF16)
    wcol[...] = dot(picked, jnp.ones((128, 128), BF16))
    for t in range(2):
        to_opposite(t).wait_recv()
        lay(3 + t, far.at[t], None)
        swap(3 + t, 0, 0)
        swap(3 + t, 1, 0)
    for t in range(2):
        arrival(t, 1)
    for t in range(2):
        for h in range(2):
            forward(3 + t, h)
    for t in range(2):
        from_sib(t, 0)
        from_sib(t, 1)
    for t in range(2):
        arrival(t, 2)
    source, slot = slot_of(iota((lines, slots), 1))
    row = iota((lines, slots), 0)
    major = where_block(source, True, side) * ROWS
    places[0] = ones_where(row == major + slot)
    places[1] = ones_where(row == source * ROWS + slot)
    places[2] = ones_where(row == major + CAP)
    for t in range(2):
        farthest(t)
        from_sib(t, 2)
    for t in range(2):
        arrival(t, 3)
    for t in range(2):
        from_sib(t, last)
        from_sib(t, 3)

    for g in range(slots // 80):
        rows = pl.ds(80 * g, 80)
        gate, up, back = acc[rows, :128], acc[rows, 128:], acch[rows, :]
        w = wcol[rows, :]
        sigma = jax.nn.sigmoid(gate)
        act = gate * sigma
        product = act * up
        scaled = w * back
        bg[rows, :128] = (scaled * up * sigma * (1.0 + gate * (1.0 - sigma))).astype(BF16)
        bg[rows, 128:] = (scaled * act).astype(BF16)
        acch[rows, :] = product.astype(BF16).astype(F32) * back
        wcol[rows, :] = w * product

    def pair(k):
        return rcopy(pout.at[k], pin.at[k], pair_s.at[k], pair_r.at[k], "tp", sib)

    def calc(k):
        def part(q):
            columns = pl.ds(pl.multiple_of(q * feat, feat), feat)
            return dot(bg[...], w2[:, columns]).astype(BF16)

        pout[k] = part(chunk(k, False))
        pair(k).start()
        pown[k] = part(chunk(k, True))

    def calc_pair(k):
        def one(i, _):
            calc(k + i * (nz - 2 * k))
            return 0

        lax.fori_loop(0, 2, one, 0)

    def put(k, h, arrived):
        rows = pl.ds(h * half_rows, half_rows)
        value = pown[k, rows, :].astype(F32) + pin[k, rows, :].astype(F32)
        if arrived is not None:
            value = value + arrived[rows, :].astype(F32)
        sbuf[k, rows, :] = value.astype(BF16)

    def sum_right(k, h):
        return rcopy(
            half(sbuf.at[k], h), half(arr_r.at[k - 1], h), rs_rs.at[k - 1, h], rs_rr.at[k - 1, h], "tp", right
        )

    def sum_left(k, h):
        return rcopy(
            half(sbuf.at[nz - k], h), half(arr_l.at[k - 1], h), rs_ls.at[k - 1, h], rs_lr.at[k - 1, h], "tp", left
        )

    def tell(i, _):
        rcopy(cb.at[tp], cb.at[tp], cb_s, cb_r, "tp", lax.rem(tp + i, n_tp)).start()
        return 0

    def lay_sums(t, total, more):
        for h in range(2):
            laid = dot(places[h], total[:, 128 * h : 128 * h + 128])
            if h == 0 and more is not None:
                laid = laid + more
            s1[t, h] = laid.astype(BF16).reshape(side, side * ROWS, 128)
            swap(t, h, 0)

    calc_pair(last - 1)
    calc(last)
    for k in range(last - 1, 0, -1):
        first = k == last - 1
        for h in range(2):
            if first and h == 0:
                pair(k).wait_recv()
            elif not first:
                if h == 0:
                    pair(k).wait_recv()
                sum_right(k + 1, 1 - h).wait_recv()
            put(k, 1 - h, None if first else arr_r.at[k])
            sum_right(k, 1 - h).start()
            if h == 0:
                pair(nz - k).wait_recv()
            if not first:
                sum_left(k + 1, h).wait_recv()
            put(nz - k, h, None if first else arr_l.at[k])
            sum_left(k, h).start()
            if h == 0 and not first:
                if k > 1:
                    calc_pair(k - 1)
                else:
                    calc(0)
        if first:
            calc_pair(k - 1)
            cb[tp, :, :slots] = dot(jnp.ones((8, 128), F32), acch[...], NT, lax.Precision.HIGHEST)
            lax.fori_loop(1, n_tp, tell, 0)
            pair(last).wait_recv()
            lay_sums(5, (pown[last].astype(F32) + pin[last].astype(F32)).astype(BF16), None)
        elif k == 2:
            for h in range(2):
                forward(5, h)

    def down(q, _):
        columns = pl.ds(pl.multiple_of(q * feat, feat), feat)
        gd[:, columns] = dot(wt[...], fdy[q])[:hid].astype(BF16)
        return 0

    some = pl.ds(0, n_tp - 1)
    comb_all = rcopy(cb.at[some], cb.at[some], cb_s, cb_r, "tp", right)
    comb_all.wait_recv()
    comb_sum = jnp.sum(cb[...], axis=0)[:1, :slots]
    values = (places[2].astype(F32) * comb_sum).astype(BF16)
    _, slot_here = slot_of(iota((slots, 128), 0))
    extra = dot(values, ones_where(slot_here == iota((slots, 128), 1)))
    wt[...] = wcol[...].T.astype(BF16)
    pair(0).wait_recv()
    for h in (1, 0):
        sum_right(1, h).wait_recv()
        sum_left(1, h).wait_recv()
    total = pown[0].astype(F32) + pin[0].astype(F32) + arr_r[0].astype(F32) + arr_l[0].astype(F32)
    lay_sums(2, total.astype(BF16), extra)
    for h in range(2):
        swapped(5, h, 1).wait_recv()
        far_out[:, 128 * h : 128 * h + 128] = dot(hot[1 - h], r2[5, h].reshape(lines, 128), TN)
    cross = rcopy(far_out, far_in, far_s.at[2], far_r.at[2], "tp", opposite)
    cross.start()
    lax.fori_loop(0, n_tp // 2, down, 0)
    for h in range(2):
        forward(2, h)
    lax.fori_loop(n_tp // 2, n_tp, down, 0)
    out = pltpu.make_async_copy(gd, gdown, gd_sem)
    out.start()

    cross.wait_recv()
    for h in range(2):
        swapped(2, h, 1).wait_recv()
        back = r2[2, h].reshape(lines, 128)
        summed = dot(hot[1 - h], back, TN) + far_in[:, 128 * h : 128 * h + 128]
        dtok[:, 128 * h : 128 * h + 128] = summed.astype(BF16)
        if h == 0:
            column = iota((n_ep, lines), 1)
            told = dot(ones_where(iota((n_ep, lines), 0) * ROWS + CAP == column), back)
    by_expert = jnp.zeros((n_ep, tokens), F32)
    for k in range(CAP):
        by_expert = jnp.where(code[...] == k, told[:, k : k + 1], by_expert)
    for k in range(ids.shape[0]):
        hit = ids[k : k + 1, :] == expert
        dcomb[k : k + 1, :] = jnp.sum(jnp.where(hit, by_expert, 0.0), axis=0, keepdims=True)

    for t in range(6):
        for h in range(2):
            for phase in range(2):
                swapped(t, h, phase).wait_send()
    for t in range(2):
        to_opposite(t).wait_send()
        for j in range(last - 1):
            for h in range(2):
                to_right(t, j, h, mine).wait_send()
                to_left(t, j, h, mine).wait_send()
        for i in range(nz):
            to_sib(t, i, mine).wait_send()
    comb_all.wait_send()
    for k in range(nz):
        pair(k).wait_send()
    for k in range(1, last):
        for h in range(2):
            sum_right(k, h).wait_send()
            sum_left(k, h).wait_send()
    cross.wait_send()
    out.wait()


def hand_over(tokens, combine, down, tokens_out, combine_out, down_out, a, b, c, in_sems, out_sems):
    part = down.shape[0] // 3
    moves = [(tokens, a, tokens_out), (combine, b, combine_out)]
    for i in range(3):
        rows = pl.ds(i * part, part)
        moves.append((down.at[rows], c.at[rows], down_out.at[rows]))
    inward = [pltpu.make_async_copy(x, y, in_sems.at[i]) for i, (x, y, _) in enumerate(moves)]
    outward = [pltpu.make_async_copy(y, z, out_sems.at[i]) for i, (_, y, z) in enumerate(moves)]
    for copy in inward:
        copy.start()
    for first, second in zip(inward, outward):
        first.wait()
        second.start()
    for copy in outward:
        copy.wait()


def per_device(n_ep, n_tp, tokens, grad_out, combine, expert_ids, w_gate, w_up, w_down):
    tok_count, feat = tokens.shape
    top = expert_ids.shape[1]
    hid, width = w_down.shape[1:]
    slots = n_ep * CAP
    nz = n_tp // 2
    side = math.isqrt(n_ep)
    vmem = pl.BlockSpec(memory_space=pltpu.VMEM)
    anyw = pl.BlockSpec(memory_space=pl.ANY)
    dma = pltpu.SemaphoreType.DMA
    blocks = pltpu.VMEM((6, 2, side, side * ROWS, 128), BF16)
    chunks = pltpu.VMEM((n_tp, slots, feat), BF16)
    parts = pltpu.VMEM((nz, slots, feat), BF16)
    results = pl.pallas_call(
        functools.partial(kernel, n_ep, n_tp),
        out_shape=(
            jax.ShapeDtypeStruct((tok_count, feat), BF16),
            jax.ShapeDtypeStruct((top, tok_count), F32),
            jax.ShapeDtypeStruct((hid, width), BF16),
        ),
        in_specs=[vmem] * 2 + [anyw] * 5,
        out_specs=(vmem, vmem, anyw),
        scratch_shapes=[
            pltpu.VMEM((tok_count, feat), BF16),
            pltpu.VMEM((tok_count, feat), BF16),
            pltpu.VMEM((2, tok_count, feat), BF16),
            pltpu.VMEM((256, width), BF16),
            pltpu.VMEM((128, width), BF16),
            pltpu.VMEM((2, n_ep * ROWS, tok_count), BF16),
            pltpu.VMEM((n_ep, tok_count), F32),
            pltpu.VMEM((3, slots, n_ep * ROWS), BF16),
            pltpu.VMEM((3, n_ep * ROWS, slots), BF16),
            blocks,
            blocks,
            blocks,
            blocks,
            chunks,
            chunks,
            pltpu.VMEM((slots, 256), F32),
            pltpu.VMEM((slots, 128), F32),
            pltpu.VMEM((slots, 128), F32),
            pltpu.VMEM((slots, 256), BF16),
            pltpu.VMEM((128, slots), BF16),
            pltpu.VMEM((n_tp, 8, 384), F32),
            parts,
            parts,
            parts,
            parts,
            pltpu.VMEM((nz // 2, slots, feat), BF16),
            pltpu.VMEM((nz // 2, slots, feat), BF16),
            pltpu.VMEM((hid, width), BF16),
            dma((5,)),
            dma((6, 2, 2)),
            dma((6, 2, 2)),
            dma((2, nz // 2 - 1, 2)),
            dma((2, nz // 2 - 1, 2)),
            dma((2, nz // 2 - 1, 2)),
            dma((2, nz // 2 - 1, 2)),
            dma((2, nz)),
            dma((2, nz)),
            dma((nz,)),
            dma((nz,)),
            dma((nz // 2, 2)),
            dma((nz // 2, 2)),
            dma((nz // 2, 2)),
            dma((nz // 2, 2)),
            dma,
            dma,
            dma,
            dma((3,)),
            dma((3,)),
            pltpu.VMEM((tok_count, feat), F32),
            pltpu.VMEM((tok_count, feat), F32),
        ],
        compiler_params=pltpu.CompilerParams(
            collective_id=0, has_side_effects=True, vmem_limit_bytes=60 * 1024 * 1024
        ),
    )(expert_ids.T, combine.T, tokens, grad_out, w_gate[0].T, w_up[0].T, w_down[0])
    d_tokens, d_combine, down = pl.pallas_call(
        hand_over,
        out_shape=tuple(jax.ShapeDtypeStruct(r.shape, r.dtype) for r in results),
        in_specs=[anyw] * 3,
        out_specs=(anyw,) * 3,
        scratch_shapes=[pltpu.VMEM(r.shape, r.dtype) for r in results] + [dma((5,)), dma((5,))],
        compiler_params=pltpu.CompilerParams(vmem_limit_bytes=60 * 1024 * 1024),
    )(*results)
    return d_tokens, d_combine.T, down[None]


def solution(mesh):
    placed = (
        P("ep", "tp"),
        P("ep", "tp"),
        P("ep", None),
        P("ep", None),
        P("ep", None, "tp"),
        P("ep", None, "tp"),
        P("ep", "tp", None),
    )
    return jax.shard_map(
        functools.partial(per_device, mesh.shape["ep"], mesh.shape["tp"]),
        mesh=mesh,
        in_specs=placed,
        out_specs=(P("ep", "tp"), P("ep", None), P("ep", "tp", None)),
        check_vma=False,
    )
```
